512 devices in a mesh: row: 32 (over y, x), col: 16 (over z, core).
Axes of the slice: x: 4, y: 8, z: 8, core: 2. Of those that a mesh axis runs over, the one named last changes fastest.
Arguments:
- positions: float32 [3, 16384], P(None, ('row', 'col')), may hold values from 0 to 1
- atom_types: int32 [16384], P(('row', 'col')), may hold values from 0 to 4
- alpha_table: float32 [5], replicated, may hold values from 0.2 to 0.6
- omega_table: float32 [5], replicated, may hold values from 0.4 to 1
- radius_table: float32 [5], replicated, may hold values from 0.8 to 1.2
- frequencies: float32 [8], replicated, may hold values from 0.05 to 0.8
- field: float32 [3, 8, 16384], P(None, None, ('row', 'col')), may hold values from -36 to 36
- start_dipoles: float32 [3, 8, 16384], P(None, None, ('row', 'col')), may hold values from -1.2 to 1.2
Outputs:
- dipoles: float32 [3, 8, 16384], P(None, None, ('row', 'col'))
- residual: float32 [3, 8, 16384], P(None, None, ('row', 'col'))
The draws below stay inside these ranges and needn't reach their ends.
All inputs are finite; a program needn't handle non-finite values.
Results may differ from the reference program's by a relative error of at most 0.0003.
Values sent between devices are 32-bit elements; how exact they have to be, the bound alone decides.
A program may use at most 64 MiB of HBM per device.

```python
import math
import jax
import jax.numpy as jnp
from jax import lax

NFREQ = 8
NTYPES = 5
ITERS = 3
ROW_ATOMS = 512
ATOMS = 16384


def draw_field(key, part):
    key = jax.random.fold_in(key, 7)
    key_values, key_spread = jax.random.split(key, 2)
    rising = 3.0 ** (jnp.arange(ATOMS, dtype=jnp.float32) / ATOMS)
    spread = jnp.exp(jax.random.uniform(key_spread, (ATOMS,), jnp.float32, 0.0, math.log(10.0)))
    values = jnp.clip(jax.random.normal(key_values, (3, NFREQ, ATOMS), jnp.float32), -4.0, 4.0)
    return 0.3 * values * (spread * rising)[None, None, :]


def place_ends(drawn, rng, low, top_value):
    longest = drawn.shape.index(max(drawn.shape))
    spots = []
    for shift in (0, 1):
        where = [jax.random.randint(jax.random.fold_in(rng, axis), (), 0, length) for axis, length in enumerate(drawn.shape)]
        where[longest] = (where[longest] + shift) % drawn.shape[longest]
        spots.append(tuple(where))
    return drawn.at[spots[0]].set(low).at[spots[1]].set(top_value)


def block_scale(stream_key, shape, cuts, least, top_value):
    level = 1.0
    for dim, blocks in cuts:
        steps = jax.random.uniform(jax.random.fold_in(jax.random.fold_in(stream_key, 6), dim), (blocks,), jnp.float32, least / len(cuts), top_value / len(cuts))
        level = level * jnp.repeat(jnp.exp(steps), shape[dim] // blocks).reshape((-1,) + (1,) * (len(shape) - 1 - dim))
    return level


def scatter_about(own_key, dims, scale, limit, shards=(), held_as=jnp.bfloat16):
    drawn = scale * jax.random.normal(own_key, dims, jnp.float32)
    if shards:
        drawn = drawn * block_scale(own_key, dims, shards, -0.22, 0.18)
    return jnp.clip(drawn, -limit, limit).astype(held_as)


def setup_inputs(seed: int = 0) -> dict:
    key_list = jax.random.split(jax.random.key(seed), 9)
    return {
        "positions": jnp.clip(1.0 * jax.random.uniform(key_list[0], (3, ATOMS), jnp.float32) ** block_scale(key_list[0], (3, ATOMS), ((1, 512),), -0.2, 0.2), 0.0, 1.0),
        "atom_types": place_ends(jax.random.randint(key_list[1], (ATOMS,), 0, NTYPES), jax.random.fold_in(key_list[1], 1), 0, NTYPES - 1).astype(jnp.int32),
        "alpha_table": jnp.clip(jnp.exp(jax.random.uniform(key_list[2], (NTYPES,), jnp.float32, math.log(0.2), math.log(0.6))), 0.2, 0.6),
        "omega_table": jnp.clip(jnp.exp(jax.random.uniform(key_list[3], (NTYPES,), jnp.float32, math.log(0.4), math.log(1.0))), 0.4, 1.0),
        "radius_table": jnp.clip(jnp.exp(jax.random.uniform(key_list[4], (NTYPES,), jnp.float32, math.log(0.8), math.log(1.2))), 0.8, 1.2),
        "frequencies": jnp.clip(jnp.exp(jax.random.uniform(key_list[5], (NFREQ,), jnp.float32, math.log(0.05), math.log(0.8))), 0.05, 0.8),
        "field": draw_field(jax.random.fold_in(key_list[8], 71), 0),
        "start_dipoles": scatter_about(key_list[7], (3, NFREQ, ATOMS), 0.2, 1.2, ((2, 512),), jnp.float32),
    }


PRECISE = lax.Precision.HIGHEST

def tensor_block(column_sites, row_sites):
    offsets = column_sites[:3, :, None] - row_sites[:3, None, :]
    reach = column_sites[3][:, None] + row_sites[3][None, :]
    square_dist = offsets[0] * offsets[0] + offsets[1] * offsets[1] + offsets[2] * offsets[2] + reach * reach
    inverse = lax.rsqrt(square_dist)
    inverse_cube = inverse * inverse * inverse
    inverse_fifth = inverse_cube * inverse * inverse
    identity = jnp.eye(3, dtype=jnp.float32)
    dyadic = -3.0 * offsets[:, None] * offsets[None, :] * inverse_fifth
    return dyadic + identity[:, :, None, None] * inverse_cube

def reference(positions, atom_types, alpha_table, omega_table, radius_table, frequencies, field, start_dipoles):
    side = (10.0 * ATOMS) ** (1.0 / 3.0)
    base_alpha = alpha_table[atom_types]
    omega = omega_table[atom_types]
    radius = radius_table[atom_types]
    diagonal = (1.0 + (frequencies[:, None] / omega[None, :]) ** 2) / base_alpha[None, :]
    sites = jnp.concatenate([positions * side, radius[None, :]], 0)
    labels = jnp.arange(ATOMS, dtype=jnp.int32)
    block_rows = math.gcd(ROW_ATOMS, 256)
    blocks = ATOMS // block_rows

    def couple(vector):

        def one_block(number):
            first = number * block_rows
            row_sites = lax.dynamic_slice_in_dim(sites, first, block_rows, 1)
            row_labels = first + jnp.arange(block_rows, dtype=jnp.int32)
            kept = (labels[:, None] != row_labels[None, :]).astype(jnp.float32)
            tensor = tensor_block(sites, row_sites) * kept
            return jnp.einsum('bfj,abji->afi', vector, tensor, precision=PRECISE)
        parts = lax.map(one_block, jnp.arange(blocks, dtype=jnp.int32))
        return jnp.moveaxis(parts, 0, 2).reshape(3, NFREQ, ATOMS)

    def apply(vector):
        return diagonal * vector + couple(vector)

    def inner(left, right):
        return lax.optimization_barrier(jnp.sum(left * right, axis=(0, 2)))
    dipoles = start_dipoles
    residual = field - apply(dipoles)
    scaled = residual / diagonal
    direction = scaled
    norm_now = inner(residual, scaled)
    for turn in range(ITERS):
        image = apply(direction)
        length = norm_now / inner(direction, image)
        dipoles = dipoles + length[None, :, None] * direction
        residual = residual - length[None, :, None] * image
        scaled = residual / diagonal
        norm_next = inner(residual, scaled)
        direction = scaled + (norm_next / norm_now)[None, :, None] * direction
        norm_now = norm_next
    return (dipoles, residual)
```

```python
import functools

import jax
import jax.numpy as jnp
from jax import lax
from jax.experimental import pallas as pl
from jax.experimental.pallas import tpu as pltpu
from jax.sharding import PartitionSpec as P

MESH = pl.DeviceIdType.MESH
F32, BF16 = jnp.float32, jnp.bfloat16
APPLICATIONS = 4
PAIRS = ((0, 0), (1, 1), (2, 2), (0, 1), (0, 2), (1, 2))
LANES = 128


def pick(indices, table, count):
    value = jnp.full(indices.shape, table[0], F32)
    for number in range(1, count):
        value = jnp.where(indices == number, table[number], value)
    return value


def kernel(
    rows, cols, piece, side,
    positions, types, alphas, omegas, radii, frequencies, field, start,
    dipoles_out, residual_out,
    gathered, partial, landed, sites, own_sites, coupling, tall, wide, sums,
    gather_send, gather_recv, sites_send, sites_recv, fold_send, fold_recv, sum_send, sum_recv,
):
    nfreq, ntypes = frequencies.shape[0], alphas.shape[0]
    row, col = lax.axis_index("row"), lax.axis_index("col")

    barrier = pltpu.get_barrier_semaphore()

    def greet_row(k, _):
        pl.semaphore_signal(barrier, inc=1, device_id=(lax.rem(row + k, rows), col), device_id_type=MESH)
        return 0

    def greet_col(k, _):
        pl.semaphore_signal(barrier, inc=1, device_id=(row, lax.rem(col + k, cols)), device_id_type=MESH)
        return 0

    lax.fori_loop(1, rows, greet_row, 0)
    lax.fori_loop(1, cols, greet_col, 0)

    def send_row(source, target, send_sem, recv_sem):
        def one(k, _):
            pltpu.make_async_remote_copy(
                src_ref=source, dst_ref=target, send_sem=send_sem, recv_sem=recv_sem,
                device_id=(lax.rem(row + k, rows), col), device_id_type=MESH,
            ).start()
            return 0

        lax.fori_loop(1, rows, one, 0)

    def send_col(source_of, target, send_sem, recv_sem):
        def one(k, _):
            peer = lax.rem(col + k, cols)
            pltpu.make_async_remote_copy(
                src_ref=source_of(peer), dst_ref=target, send_sem=send_sem, recv_sem=recv_sem,
                device_id=(row, peer), device_id_type=MESH,
            ).start()
            return 0

        lax.fori_loop(1, cols, one, 0)

    def wait_for(buffer, count, sem):
        view = buffer.at[pl.ds(0, count)]
        pltpu.make_async_copy(view, view, sem).wait()

    def packed(ref):
        return jnp.concatenate([ref[0], ref[1], ref[2]], axis=1)

    lane = lax.broadcasted_iota(jnp.int32, (nfreq, LANES), 1)
    used = lane < 3 * piece
    level = lax.broadcasted_iota(jnp.int32, (nfreq, LANES), 0)
    kinds = types[...]
    radius = pick(kinds, radii, ntypes)
    place = positions[...] * side
    pad = jnp.zeros((nfreq - 4, piece), F32)
    site = jnp.concatenate([place, radius, pad], axis=0)
    start_packed = packed(start)
    message = jnp.concatenate([start_packed, site], axis=1)
    kinds_packed = jnp.broadcast_to(jnp.concatenate([kinds] * (LANES // piece), axis=1), (nfreq, LANES))
    omega = pick(kinds_packed, omegas, ntypes)
    alpha = pick(kinds_packed, alphas, ntypes)
    ratio = pick(level, frequencies, nfreq) / omega
    diagonal = (1.0 + ratio * ratio) / alpha
    zeros_tail = jnp.zeros((nfreq, LANES - 3 * piece), F32)
    start_full = jnp.concatenate([start_packed, zeros_tail], axis=1)
    field_full = jnp.concatenate([packed(field), zeros_tail], axis=1)

    gathered[0, row] = message
    sites[col] = message
    pl.semaphore_wait(barrier, rows + cols - 2)
    send_row(gathered.at[0, row], gathered.at[0, row], gather_send.at[0], gather_recv.at[0])
    send_col(lambda peer: sites.at[col], sites.at[col], sites_send, sites_recv)

    wait_for(sites, cols - 1, sites_recv)
    for c in range(cols):
        own_sites[:, c * piece:(c + 1) * piece] = sites[c][:, 3 * piece:]
    wait_for(gathered.at[0], rows - 1, gather_recv.at[0])

    width = cols * piece

    def build(s, _):
        turned = gathered[0, s].T[3 * piece:, :]
        base = pl.multiple_of(s * piece, piece)
        column = [jnp.broadcast_to(turned[:, q:q + 1], (piece, LANES)) for q in range(4)]
        for n in range(width // LANES):
            span = slice(n * LANES, (n + 1) * LANES)
            offset = [column[q] - own_sites[q:q + 1, span] for q in range(3)]
            reach = column[3] + own_sites[3:4, span]
            square = offset[0] * offset[0] + offset[1] * offset[1] + offset[2] * offset[2] + reach * reach
            inverse = lax.rsqrt(square)
            second = inverse * inverse
            cube = second * inverse
            fifth = -3.0 * (cube * second)
            weighted = [offset[q] * fifth for q in range(3)]
            for number, (a, b) in enumerate(PAIRS):
                value = weighted[a] * offset[b]
                if a == b:
                    value = value + cube
                high = value.astype(BF16)
                coupling[number, 0, pl.ds(base, piece), span] = high
                coupling[number, 1, pl.ds(base, piece), span] = (value - high.astype(F32)).astype(BF16)
        return 0

    lax.fori_loop(0, rows, build, 0)

    base = pl.multiple_of(row * piece, piece)
    group = LANES // piece
    span = pl.ds(pl.multiple_of((col // group) * LANES, LANES), LANES)
    shift = lax.rem(col, group) * piece
    apart = (
        lax.broadcasted_iota(jnp.int32, (piece, LANES), 0) + shift
        != lax.broadcasted_iota(jnp.int32, (piece, LANES), 1)
    )
    for number in range(len(PAIRS)):
        for part in range(2):
            block = coupling[number, part, pl.ds(base, piece), span].astype(F32)
            coupling[number, part, pl.ds(base, piece), span] = jnp.where(apart, block, 0.0).astype(BF16)

    def apply(turn):
        for a in range(3):
            for t in range(rows * piece // LANES):
                tall[a, :, t * LANES:(t + 1) * LANES] = jnp.concatenate(
                    [gathered[turn, t * group + q][:, a * piece:(a + 1) * piece] for q in range(group)], axis=1
                )
        highs, lows = [], []
        for a in range(3):
            value = tall[a]
            high = value.astype(BF16).astype(F32)
            highs.append(high)
            lows.append(value - high)
        out = [jnp.zeros((nfreq, width), F32) for _ in range(3)]

        def dot(left, number, part):
            return jnp.dot(
                jnp.concatenate(left, axis=0).astype(BF16), coupling[number, part], preferred_element_type=F32
            )

        for number, (a, b) in enumerate(PAIRS):
            if a == b:
                main = dot([highs[a], lows[a]], number, 0)
                rest = dot([highs[a], lows[a]], number, 1)
                out[a] = out[a] + (main[:nfreq] + (main[nfreq:] + rest[:nfreq]))
            else:
                main = dot([highs[b], lows[b], highs[a], lows[a]], number, 0)
                rest = dot([highs[b], highs[a]], number, 1)
                out[a] = out[a] + (main[:nfreq] + (main[nfreq:2 * nfreq] + rest[:nfreq]))
                out[b] = out[b] + (main[2 * nfreq:3 * nfreq] + (main[3 * nfreq:] + rest[nfreq:]))
        for a in range(3):
            wide[a] = out[a]
        for c in range(cols):
            cut = slice(c * piece, (c + 1) * piece)
            partial[turn, c] = jnp.concatenate([wide[0, :, cut], wide[1, :, cut], wide[2, :, cut], zeros_tail], axis=1)
        landed[turn, col] = partial[turn, col]
        send_col(lambda peer: partial.at[turn, peer], landed.at[turn, col], fold_send.at[turn], fold_recv.at[turn])
        wait_for(landed.at[turn], cols - 1, fold_recv.at[turn])
        total = landed[turn, 0]
        for c in range(1, cols):
            total = total + landed[turn, c]
        return total

    def spread(turn, value):
        gathered[turn, row] = value
        send_row(gathered.at[turn, row], gathered.at[turn, row], gather_send.at[turn], gather_recv.at[turn])
        wait_for(gathered.at[turn], rows - 1, gather_recv.at[turn])

    powers = [field_full - diagonal * start_full - apply(0)]
    scaled = []
    for turn in range(1, APPLICATIONS):
        scaled.append(powers[-1] / diagonal)
        spread(turn, scaled[-1])
        powers.append(apply(turn))

    moments = jnp.zeros((nfreq, LANES), F32)
    for k, (i, j) in enumerate(((0, 0), (0, 1), (1, 1), (1, 2), (2, 2), (2, 3))):
        local = jnp.sum(jnp.where(used, scaled[i] * powers[j], 0.0), axis=1, keepdims=True)
        moments = jnp.where(lane == k, local, moments)
    sums[0, row] = moments
    send_row(sums.at[0, row], sums.at[0, row], sum_send.at[0], sum_recv.at[0])
    wait_for(sums.at[0], rows - 1, sum_recv.at[0])
    total = sums[0, 0]
    for r in range(1, rows):
        total = total + sums[0, r]
    sums[1, col] = total
    send_col(lambda peer: sums.at[1, col], sums.at[1, col], sum_send.at[1], sum_recv.at[1])
    wait_for(sums.at[1], cols - 1, sum_recv.at[1])
    total = sums[1, 0]
    for c in range(1, cols):
        total = total + sums[1, c]

    m = [jnp.broadcast_to(total[:, k:k + 1], (nfreq, LANES)) for k in range(6)]
    a0 = m[1] / m[0]
    h0 = m[0]
    h1 = m[2] - a0 * m[1]
    a1 = (m[3] - 2.0 * a0 * m[2] + a0 * a0 * m[1]) / h1
    b1 = h1 / h0
    c1 = -(a0 + a1)
    c0 = a0 * a1 - b1
    h2 = m[4] + c1 * m[3] + c0 * m[2]
    a2 = (m[5] + c1 * m[4] + c0 * m[3]) / h2 + c1
    b2 = h2 / h1
    e2 = c1 - a2
    e1 = c0 - a2 * c1 - b2
    e0 = b2 * a0 - a2 * c0
    top = 1.0 / (e2 - 1.0 - e1 + e0)
    p3, p2, p1, p0 = top, e2 * top, e1 * top, e0 * top
    s2 = -p3
    s1 = -p2 - s2
    s0 = -p1 - s1
    residual = p0 * powers[0] + p1 * powers[1] + p2 * powers[2] + p3 * powers[3]
    dipoles = start_full + (s0 * scaled[0] + s1 * scaled[1] + s2 * scaled[2])
    for a in range(3):
        dipoles_out[a] = dipoles[:, a * piece:(a + 1) * piece]
        residual_out[a] = residual[:, a * piece:(a + 1) * piece]

    for turn in range(APPLICATIONS):
        wait_for(gathered.at[turn], rows - 1, gather_send.at[turn])
        wait_for(landed.at[turn], cols - 1, fold_send.at[turn])
    wait_for(sites, cols - 1, sites_send)
    wait_for(sums.at[0], rows - 1, sum_send.at[0])
    wait_for(sums.at[1], cols - 1, sum_send.at[1])


def solution(mesh):
    rows, cols = mesh.shape["row"], mesh.shape["col"]

    def shards(positions, atom_types, alpha_table, omega_table, radius_table, frequencies, field, start_dipoles):
        piece, nfreq = positions.shape[1], frequencies.shape[0]
        side = (10.0 * piece * rows * cols) ** (1.0 / 3.0)
        vmem = pl.BlockSpec(memory_space=pltpu.VMEM)
        smem = pl.BlockSpec(memory_space=pltpu.SMEM)
        tile = (nfreq, LANES)
        dma = pltpu.SemaphoreType.DMA
        return pl.pallas_call(
            functools.partial(kernel, rows, cols, piece, side),
            out_shape=(jax.ShapeDtypeStruct(field.shape, F32),) * 2,
            in_specs=[vmem, vmem, smem, smem, smem, smem, vmem, vmem],
            out_specs=(vmem, vmem),
            scratch_shapes=[
                pltpu.VMEM((APPLICATIONS, rows) + tile, F32),
                pltpu.VMEM((APPLICATIONS, cols) + tile, F32),
                pltpu.VMEM((APPLICATIONS, cols) + tile, F32),
                pltpu.VMEM((cols,) + tile, F32),
                pltpu.VMEM((nfreq, cols * piece), F32),
                pltpu.VMEM((len(PAIRS), 2, rows * piece, cols * piece), BF16),
                pltpu.VMEM((3, nfreq, rows * piece), F32),
                pltpu.VMEM((3, nfreq, cols * piece), F32),
                pltpu.VMEM((2, rows) + tile, F32),
                dma((APPLICATIONS,)), dma((APPLICATIONS,)),
                dma, dma,
                dma((APPLICATIONS,)), dma((APPLICATIONS,)),
                dma((2,)), dma((2,)),
            ],
            compiler_params=pltpu.CompilerParams(
                collective_id=0, has_side_effects=True, vmem_limit_bytes=48 * 1024 * 1024
            ),
        )(
            positions, atom_types.reshape(1, piece), alpha_table, omega_table, radius_table, frequencies,
            field, start_dipoles,
        )

    placed = (
        P(None, ("row", "col")),
        P(("row", "col")),
        P(),
        P(),
        P(),
        P(),
        P(None, None, ("row", "col")),
        P(None, None, ("row", "col")),
    )
    return jax.shard_map(
        shards,
        mesh=mesh,
        in_specs=placed,
        out_specs=(P(None, None, ("row", "col")), P(None, None, ("row", "col"))),
        check_vma=False,
    )
```

```python
import functools

import jax
import jax.numpy as jnp
from jax import lax
from jax.experimental import pallas as pl
from jax.experimental.pallas import tpu as pltpu
from jax.sharding import PartitionSpec as P

MESH = pl.DeviceIdType.MESH
F32, BF16 = jnp.float32, jnp.bfloat16
APPLICATIONS = 4
PAIRS = ((0, 0), (1, 1), (2, 2), (0, 1), (0, 2), (1, 2))
LANES = 128
TILE = 8
TILE_ORDER = (0, 1, 2, 3)
ROW_MINOR = 4
COL_MINOR = 2
MOMENTS = ((0, 0), (0, 1), (1, 1), (1, 2), (2, 2))


def pick(indices, table, count):
    value = jnp.full(indices.shape, table[0], F32)
    for number in range(1, count):
        value = jnp.where(indices == number, table[number], value)
    return value


def hops(step, length):
    return min(step, length - step)


def nearest_first(count, minor, hop_minor):
    major = count // minor
    offsets = [(far, near) for far in range(major) for near in range(minor)]
    return sorted(offsets, key=lambda o: (hops(o[0], major) + hop_minor * hops(o[1], minor), o))


def turned(me, count, minor):
    major = count // minor
    high, low = lax.div(me, minor), lax.rem(me, minor)
    highs = [lax.rem(high + step, major) * minor for step in range(major)]
    lows = [lax.rem(low + step, minor) for step in range(minor)]
    return highs, lows


def kernel(
    rows, cols, piece, side,
    positions_hbm, types_hbm, alphas_hbm, omegas_hbm, radii_hbm, frequencies_hbm, field_hbm, start_hbm,
    dipoles_out, residual_out,
    positions, types, alphas, omegas, radii, frequencies, field, start,
    gathered, partial, landed, sites, mates, own_sites, coupling, sums,
    load_sem, gather_send, gather_recv, sites_send, sites_recv, fold_send, fold_recv,
    mates_send, mates_recv, sum_send, sum_recv,
):
    nfreq, ntypes = frequencies.shape[0], alphas.shape[0]
    row, col = lax.axis_index("row"), lax.axis_index("col")
    tiles = rows // TILE
    group = LANES // piece
    width = cols * piece
    depth = TILE * piece

    loads = [
        pltpu.make_async_copy(source, target, load_sem.at[number])
        for number, (source, target) in enumerate((
            (positions_hbm, positions), (types_hbm, types), (alphas_hbm, alphas), (omegas_hbm, omegas),
            (radii_hbm, radii), (frequencies_hbm, frequencies), (field_hbm, field), (start_hbm, start),
        ))
    ]
    for load in loads:
        load.start()

    barrier = pltpu.get_barrier_semaphore()

    row_offsets = nearest_first(rows, ROW_MINOR, 1)
    col_offsets = nearest_first(cols, COL_MINOR, 0.5)
    row_high, row_low = turned(row, rows, ROW_MINOR)
    col_high, col_low = turned(col, cols, COL_MINOR)

    def row_peer(slot, sign):
        far, near = row_offsets[slot]
        return (row_high[sign * far % len(row_high)] + row_low[sign * near % len(row_low)], col)

    def col_peer(slot, sign):
        far, near = col_offsets[slot]
        return (row, col_high[sign * far % len(col_high)] + col_low[sign * near % len(col_low)])

    row_order = range(rows - 1, 0, -1)
    col_order = range(cols - 1, 0, -1)

    with jax.named_scope("greet"):
        for slot in row_order:
            pl.semaphore_signal(barrier, inc=1, device_id=row_peer(slot, 1), device_id_type=MESH)
        for slot in col_order:
            pl.semaphore_signal(barrier, inc=1, device_id=col_peer(slot, 1), device_id_type=MESH)

    def send_row(source, target, send_sem, recv_sem_of):
        for slot in row_order:
            pltpu.make_async_remote_copy(
                src_ref=source, dst_ref=target.at[slot], send_sem=send_sem, recv_sem=recv_sem_of(slot),
                device_id=row_peer(slot, -1), device_id_type=MESH,
            ).start()

    def send_col(source_of, target, send_sem, recv_sem, sign):
        for slot in col_order:
            pltpu.make_async_remote_copy(
                src_ref=source_of(slot), dst_ref=target.at[slot], send_sem=send_sem, recv_sem=recv_sem,
                device_id=col_peer(slot, sign), device_id_type=MESH,
            ).start()

    def wait_for(buffer, count, sem):
        view = buffer.at[pl.ds(0, count)]
        pltpu.make_async_copy(view, view, sem).wait()

    def packed(ref):
        return jnp.concatenate([ref[0], ref[1], ref[2]], axis=1)

    with jax.named_scope("load"):
        for load in loads:
            load.wait()
    lane = lax.broadcasted_iota(jnp.int32, (nfreq, LANES), 1)
    level = lax.broadcasted_iota(jnp.int32, (nfreq, LANES), 0)
    kinds = types[...]
    radius = pick(kinds, radii, ntypes)
    place = positions[...] * side
    pad = jnp.zeros((nfreq - 4, piece), F32)
    site = jnp.concatenate([place, radius, pad], axis=0)
    start_packed = packed(start)
    message = jnp.concatenate([start_packed, site], axis=1)
    gathered[0, 0] = message
    sites[0] = message
    with jax.named_scope("barrier"):
        pl.semaphore_wait(barrier, rows + cols - 2)
    with jax.named_scope("first send"):
        send_col(lambda slot: sites.at[0], sites, sites_send, sites_recv, -1)
        send_row(gathered.at[0, 0], gathered.at[0], gather_send.at[0], lambda slot: gather_recv.at[0, slot // TILE])

    kinds_packed = jnp.broadcast_to(jnp.concatenate([kinds] * group, axis=1), (nfreq, LANES))
    omega = pick(kinds_packed, omegas, ntypes)
    alpha = pick(kinds_packed, alphas, ntypes)
    ratio = pick(level, frequencies, nfreq) / omega
    diagonal = (1.0 + ratio * ratio) / alpha
    inverse_diagonal = alpha / (1.0 + ratio * ratio)
    zeros_tail = jnp.zeros((nfreq, LANES - 3 * piece), F32)
    start_full = jnp.concatenate([start_packed, zeros_tail], axis=1)
    field_full = jnp.concatenate([packed(field), zeros_tail], axis=1)
    source_full = field_full - diagonal * start_full

    with jax.named_scope("sites wait"):
        wait_for(sites, cols - 1, sites_recv)
    for c in range(cols):
        own_sites[:, c * piece:(c + 1) * piece] = sites[c][:, 3 * piece:]

    def build(tile, s, _):
        turned = gathered[0, tile * TILE + s].T[3 * piece:, :]
        base = pl.multiple_of(s * piece, piece)
        column = [jnp.broadcast_to(turned[:, q:q + 1], (piece, LANES)) for q in range(4)]
        for n in range(width // LANES):
            span = slice(n * LANES, (n + 1) * LANES)
            offset = [column[q] - own_sites[q:q + 1, span] for q in range(3)]
            reach = column[3] + own_sites[3:4, span]
            square = offset[0] * offset[0] + offset[1] * offset[1] + offset[2] * offset[2] + reach * reach
            inverse = lax.rsqrt(square)
            second = inverse * inverse
            cube = second * inverse
            fifth = -3.0 * (cube * second)
            weighted = [offset[q] * fifth for q in range(3)]
            for number, (a, b) in enumerate(PAIRS):
                value = weighted[a] * offset[b]
                if a == b:
                    value = value + cube
                high = value.astype(BF16)
                coupling[tile, number, 0, pl.ds(base, piece), span] = high
                coupling[tile, number, 1, pl.ds(base, piece), span] = (value - high.astype(F32)).astype(BF16)
        return 0

    def drop_self():
        apart = (
            lax.broadcasted_iota(jnp.int32, (piece, LANES), 0) != lax.broadcasted_iota(jnp.int32, (piece, LANES), 1)
        )
        for number in range(len(PAIRS)):
            for part in range(2):
                block = coupling[0, number, part, :piece, :LANES].astype(F32)
                coupling[0, number, part, :piece, :LANES] = jnp.where(apart, block, 0.0).astype(BF16)

    def unpack(block_of, count):
        blocks = [block_of(s) for s in range(count)]
        return [
            jnp.concatenate(
                [
                    jnp.concatenate([blocks[t + q][:, a * piece:(a + 1) * piece] for q in range(group)], axis=1)
                    for t in range(0, count, group)
                ],
                axis=1,
            )
            for a in range(3)
        ]

    def apply(turn):
        main = [None] * len(PAIRS)
        rest = [None] * len(PAIRS)
        for place, tile in enumerate(TILE_ORDER):
            with jax.named_scope(f"tile {tile} wait"):
                wait_for(gathered.at[turn], TILE - 1 if tile == 0 else TILE, gather_recv.at[turn, tile])
            if turn == 0:
                with jax.named_scope("build"):
                    lax.fori_loop(0, TILE, functools.partial(build, tile), 0)
                if tile == 0:
                    drop_self()
            with jax.named_scope("matmul"):
                values = unpack(lambda s: gathered[turn, tile * TILE + s], TILE)
                highs = [value.astype(BF16).astype(F32) for value in values]
                lows = [value - high for value, high in zip(values, highs)]

                def dot(left, number, part):
                    return jnp.dot(
                        jnp.concatenate(left, axis=0).astype(BF16), coupling[tile, number, part],
                        preferred_element_type=F32,
                    )

                for number, (a, b) in enumerate(PAIRS):
                    if a == b:
                        first = dot([highs[a], lows[a]], number, 0)
                        second = dot([highs[a], lows[a]], number, 1)
                    else:
                        first = dot([highs[b], lows[b], highs[a], lows[a]], number, 0)
                        second = dot([highs[b], highs[a]], number, 1)
                    main[number] = first if place == 0 else main[number] + first
                    rest[number] = second if place == 0 else rest[number] + second
        out = [None] * 3

        def add(a, value):
            out[a] = value if out[a] is None else out[a] + value

        for number, (a, b) in enumerate(PAIRS):
            add(a, main[number][:nfreq] + (main[number][nfreq:2 * nfreq] + rest[number][:nfreq]))
            if a != b:
                add(b, main[number][2 * nfreq:3 * nfreq] + (main[number][3 * nfreq:] + rest[number][nfreq:]))
        return out

    def fold(turn, out, tail):
        for c in range(cols):
            cut = slice(c * piece, (c + 1) * piece)
            block = jnp.concatenate([out[0][:, cut], out[1][:, cut], out[2][:, cut], tail], axis=1)
            if c == 0:
                landed[turn, 0] = block
            else:
                partial[turn, c] = block
        with jax.named_scope("fold send"):
            send_col(lambda slot: partial.at[turn, slot], landed.at[turn], fold_send.at[turn], fold_recv.at[turn], 1)
        with jax.named_scope("fold wait"):
            wait_for(landed.at[turn], cols - 1, fold_recv.at[turn])
        total = landed[turn, 0]
        for c in range(1, cols):
            total = total + landed[turn, c]
        return total

    def spread(turn, value):
        gathered[turn, 0] = value
        with jax.named_scope("gather send"):
            send_row(
                gathered.at[turn, 0], gathered.at[turn], gather_send.at[turn],
                lambda slot: gather_recv.at[turn, slot // TILE],
            )

    powers = [source_full - fold(0, apply(0), zeros_tail)]
    scaled = []
    for turn in range(1, APPLICATIONS):
        scaled.append(powers[-1] * inverse_diagonal)
        spread(turn, scaled[-1])
        if turn + 1 < APPLICATIONS:
            powers.append(fold(turn, apply(turn), zeros_tail))

    last = APPLICATIONS - 1
    mates[0] = scaled[last - 1]
    send_col(lambda slot: mates.at[0], mates, mates_send, mates_recv, -1)
    moments = zeros_tail
    tail_lane = lax.broadcasted_iota(jnp.int32, zeros_tail.shape, 1)
    for k, (i, j) in enumerate(MOMENTS):
        local = jnp.sum(scaled[i] * powers[j], axis=1, keepdims=True)
        moments = jnp.where(tail_lane == k, local, moments)
    out = apply(last)
    wait_for(mates, cols - 1, mates_recv)
    own = unpack(lambda s: mates[s], cols)
    local = jnp.sum(own[0] * out[0] + own[1] * out[1] + own[2] * out[2], axis=1, keepdims=True)
    moments = jnp.where(tail_lane == len(MOMENTS), local, moments)
    folded = fold(last, out, moments)
    sums[0] = folded
    with jax.named_scope("sum"):
        send_row(sums.at[0], sums, sum_send, lambda slot: sum_recv)
        powers.append(jnp.where(lane < 3 * piece, folded, 0.0))
        wait_for(sums, rows - 1, sum_recv)
    total = sums[0]
    for r in range(1, rows):
        total = total + sums[r]

    m = [jnp.broadcast_to(total[:, 3 * piece + k:3 * piece + k + 1], (nfreq, LANES)) for k in range(6)]
    a0 = m[1] / m[0]
    h0 = m[0]
    h1 = m[2] - a0 * m[1]
    a1 = (m[3] - 2.0 * a0 * m[2] + a0 * a0 * m[1]) / h1
    b1 = h1 / h0
    c1 = -(a0 + a1)
    c0 = a0 * a1 - b1
    h2 = m[4] + c1 * m[3] + c0 * m[2]
    a2 = (m[5] + c1 * m[4] + c0 * m[3]) / h2 + c1
    b2 = h2 / h1
    e2 = c1 - a2
    e1 = c0 - a2 * c1 - b2
    e0 = b2 * a0 - a2 * c0
    top = 1.0 / (e2 - 1.0 - e1 + e0)
    p3, p2, p1, p0 = top, e2 * top, e1 * top, e0 * top
    s2 = -p3
    s1 = -p2 - s2
    s0 = -p1 - s1
    residual = p0 * powers[0] + p1 * powers[1] + p2 * powers[2] + p3 * powers[3]
    dipoles = start_full + (s0 * scaled[0] + s1 * scaled[1] + s2 * scaled[2])
    for a in range(3):
        dipoles_out[a] = dipoles[:, a * piece:(a + 1) * piece]
        residual_out[a] = residual[:, a * piece:(a + 1) * piece]

    for turn in range(APPLICATIONS):
        wait_for(gathered.at[turn], rows - 1, gather_send.at[turn])
        wait_for(landed.at[turn], cols - 1, fold_send.at[turn])
    wait_for(sites, cols - 1, sites_send)
    wait_for(mates, cols - 1, mates_send)
    wait_for(sums, rows - 1, sum_send)


def solution(mesh):
    rows, cols = mesh.shape["row"], mesh.shape["col"]

    def shards(positions, atom_types, alpha_table, omega_table, radius_table, frequencies, field, start_dipoles):
        piece, nfreq = positions.shape[1], frequencies.shape[0]
        side = (10.0 * piece * rows * cols) ** (1.0 / 3.0)
        operands = (
            positions, atom_types.reshape(1, piece), alpha_table, omega_table, radius_table, frequencies,
            field, start_dipoles,
        )
        vmem = pl.BlockSpec(memory_space=pltpu.VMEM)
        tile = (nfreq, LANES)
        dma = pltpu.SemaphoreType.DMA
        places = [pltpu.VMEM] * 2 + [pltpu.SMEM] * 4 + [pltpu.VMEM] * 2
        return pl.pallas_call(
            functools.partial(kernel, rows, cols, piece, side),
            out_shape=(jax.ShapeDtypeStruct(field.shape, F32),) * 2,
            in_specs=[pl.BlockSpec(memory_space=pltpu.HBM)] * len(operands),
            out_specs=(vmem, vmem),
            scratch_shapes=[space(array.shape, array.dtype) for space, array in zip(places, operands)] + [
                pltpu.VMEM((APPLICATIONS, rows) + tile, F32),
                pltpu.VMEM((APPLICATIONS, cols) + tile, F32),
                pltpu.VMEM((APPLICATIONS, cols) + tile, F32),
                pltpu.VMEM((cols,) + tile, F32),
                pltpu.VMEM((cols,) + tile, F32),
                pltpu.VMEM((nfreq, cols * piece), F32),
                pltpu.VMEM((rows // TILE, len(PAIRS), 2, TILE * piece, cols * piece), BF16),
                pltpu.VMEM((rows,) + tile, F32),
                dma((len(operands),)),
                dma((APPLICATIONS,)), dma((APPLICATIONS, rows // TILE)),
                dma, dma,
                dma((APPLICATIONS,)), dma((APPLICATIONS,)),
                dma, dma,
                dma, dma,
            ],
            compiler_params=pltpu.CompilerParams(
                collective_id=0, has_side_effects=True, vmem_limit_bytes=64 * 1024 * 1024
            ),
        )(*operands)

    placed = (
        P(None, ("row", "col")),
        P(("row", "col")),
        P(),
        P(),
        P(),
        P(),
        P(None, None, ("row", "col")),
        P(None, None, ("row", "col")),
    )
    return jax.shard_map(
        shards,
        mesh=mesh,
        in_specs=placed,
        out_specs=(P(None, None, ("row", "col")), P(None, None, ("row", "col"))),
        check_vma=False,
    )
```

```python
import functools

import jax
import jax.numpy as jnp
from jax import lax
from jax.experimental import pallas as pl
from jax.experimental.pallas import tpu as pltpu
from jax.sharding import PartitionSpec as P

MESH = pl.DeviceIdType.MESH
F32, BF16 = jnp.float32, jnp.bfloat16
APPLICATIONS = 4
PAIRS = ((0, 0), (1, 1), (2, 2), (0, 1), (0, 2), (1, 2))
LANES = 128
TILE = 8
ROW_MINOR = 4
COL_MINOR = 2
MOMENTS = ((0, 0), (0, 1), (1, 1), (1, 2), (2, 2))


def pick(indices, table, count):
    value = jnp.full(indices.shape, table[0], F32)
    for number in range(1, count):
        value = jnp.where(indices == number, table[number], value)
    return value


def hops(step, length):
    return min(step, length - step)


def nearest_first(count, minor, hop_minor):
    major = count // minor
    offsets = [(far, near) for far in range(major) for near in range(minor)]
    return sorted(offsets, key=lambda o: (hops(o[0], major) + hop_minor * hops(o[1], minor), o))


def turned(me, count, minor):
    major = count // minor
    high, low = lax.div(me, minor), lax.rem(me, minor)
    highs = [lax.rem(high + step, major) * minor for step in range(major)]
    lows = [lax.rem(low + step, minor) for step in range(minor)]
    return highs, lows


def kernel(
    rows, cols, piece, side,
    positions_hbm, types_hbm, alphas_hbm, omegas_hbm, radii_hbm, frequencies_hbm, field_hbm, start_hbm,
    dipoles_out, residual_out,
    positions, types, alphas, omegas, radii, frequencies, field, start,
    gathered, partial, landed, sites, mates, own_sites, columns, coupling, col_sums, row_sums,
    load_sem, gather_send, gather_recv, sites_send, sites_recv, fold_send, fold_recv,
    mates_send, mates_recv, sum_send, sum_recv,
):
    nfreq, ntypes = frequencies.shape[0], alphas.shape[0]
    row, col = lax.axis_index("row"), lax.axis_index("col")
    tiles = rows // TILE
    group = LANES // piece
    depth = TILE * piece

    loads = [
        pltpu.make_async_copy(source, target, load_sem.at[number])
        for number, (source, target) in enumerate((
            (positions_hbm, positions), (types_hbm, types), (alphas_hbm, alphas), (omegas_hbm, omegas),
            (radii_hbm, radii), (frequencies_hbm, frequencies), (field_hbm, field), (start_hbm, start),
        ))
    ]
    barrier = pltpu.get_barrier_semaphore()

    row_offsets = nearest_first(rows, ROW_MINOR, 1)
    col_offsets = nearest_first(cols, COL_MINOR, 0.5)
    row_high, row_low = turned(row, rows, ROW_MINOR)
    col_high, col_low = turned(col, cols, COL_MINOR)

    def row_peer(slot, sign):
        far, near = row_offsets[slot]
        return (row_high[sign * far % len(row_high)] + row_low[sign * near % len(row_low)], col)

    def col_peer(slot, sign):
        far, near = col_offsets[slot]
        return (row, col_high[sign * far % len(col_high)] + col_low[sign * near % len(col_low)])

    row_order = range(rows - 1, 0, -1)
    col_order = range(cols - 1, 0, -1)

    with jax.named_scope("greet"):
        for slot in row_order:
            pl.semaphore_signal(barrier, inc=1, device_id=row_peer(slot, 1), device_id_type=MESH)
        for slot in col_order:
            pl.semaphore_signal(barrier, inc=1, device_id=col_peer(slot, 1), device_id_type=MESH)

    for load in loads:
        load.start()

    def send_row(source_of, target, send_sem, recv_sem, sign, slots=row_order):
        for slot in slots:
            pltpu.make_async_remote_copy(
                src_ref=source_of(slot), dst_ref=target.at[slot], send_sem=send_sem, recv_sem=recv_sem,
                device_id=row_peer(slot, sign), device_id_type=MESH,
            ).start()

    def send_col(source, target, send_sem, recv_sem):
        for slot in col_order:
            pltpu.make_async_remote_copy(
                src_ref=source, dst_ref=target.at[slot], send_sem=send_sem, recv_sem=recv_sem,
                device_id=col_peer(slot, -1), device_id_type=MESH,
            ).start()

    def wait_for(buffer, count, sem):
        view = buffer.at[pl.ds(0, count)]
        pltpu.make_async_copy(view, view, sem).wait()

    def packed(ref):
        return jnp.concatenate([ref[0], ref[1], ref[2]], axis=1)

    with jax.named_scope("load"):
        for load in loads:
            load.wait()
    lane = lax.broadcasted_iota(jnp.int32, (nfreq, LANES), 1)
    level = lax.broadcasted_iota(jnp.int32, (nfreq, LANES), 0)
    kinds = types[...]
    radius = pick(kinds, radii, ntypes)
    place = positions[...] * side
    pad = jnp.zeros((nfreq - 4, piece), F32)
    site = jnp.concatenate([place, radius, pad], axis=0)
    start_packed = packed(start)
    message = jnp.concatenate([start_packed, site], axis=1)
    gathered[0, 0] = message
    sites[0] = message
    with jax.named_scope("barrier"):
        pl.semaphore_wait(barrier, rows + cols - 2)
    with jax.named_scope("first send"):
        send_row(lambda slot: sites.at[0], sites, sites_send, sites_recv, -1)
        send_col(gathered.at[0, 0], gathered.at[0], gather_send.at[0], gather_recv.at[0])

    kinds_packed = jnp.broadcast_to(jnp.concatenate([kinds] * group, axis=1), (nfreq, LANES))
    omega = pick(kinds_packed, omegas, ntypes)
    alpha = pick(kinds_packed, alphas, ntypes)
    ratio = pick(level, frequencies, nfreq) / omega
    diagonal = (1.0 + ratio * ratio) / alpha
    inverse_diagonal = alpha / (1.0 + ratio * ratio)
    zeros_tail = jnp.zeros((nfreq, LANES - 3 * piece), F32)
    start_full = jnp.concatenate([start_packed, zeros_tail], axis=1)
    field_full = jnp.concatenate([packed(field), zeros_tail], axis=1)
    source_full = field_full - diagonal * start_full

    def total_of(values):
        while len(values) > 1:
            values = [sum(values[k:k + 2]) for k in range(0, len(values), 2)]
        return values[0]

    def unpack(block_of, count):
        blocks = [block_of(s) for s in range(count)]
        return [
            jnp.concatenate(
                [
                    jnp.concatenate([blocks[t + q][:, a * piece:(a + 1) * piece] for q in range(group)], axis=1)
                    for t in range(0, count, group)
                ],
                axis=1,
            )
            for a in range(3)
        ]

    def prepare():
        for c in range(cols):
            across = gathered[0, c].T[3 * piece:, :]
            for q in range(4):
                columns[q, c * piece:(c + 1) * piece, :] = jnp.broadcast_to(across[:, q:q + 1], (piece, LANES))
        for r in range(rows):
            own_sites[:, r * piece:(r + 1) * piece] = sites[r][:, 3 * piece:]

    apart = (
        lax.broadcasted_iota(jnp.int32, (piece, LANES), 0) != lax.broadcasted_iota(jnp.int32, (piece, LANES), 1)
    )

    def build(chunk):
        for c in range(cols):
            base = slice(c * piece, (c + 1) * piece)
            column = [columns[q, base, :] for q in range(4)]
            for n in range(depth // LANES):
                span = slice(n * LANES, (n + 1) * LANES)
                place = slice(chunk * depth + n * LANES, chunk * depth + (n + 1) * LANES)
                offset = [column[q] - own_sites[q:q + 1, place] for q in range(3)]
                reach = column[3] + own_sites[3:4, place]
                square = offset[0] * offset[0] + offset[1] * offset[1] + offset[2] * offset[2] + reach * reach
                inverse = lax.rsqrt(square)
                second = inverse * inverse
                cube = second * inverse
                fifth = -3.0 * (cube * second)
                weighted = [offset[q] * fifth for q in range(3)]
                for number, (a, b) in enumerate(PAIRS):
                    value = weighted[a] * offset[b]
                    if a == b:
                        value = value + cube
                    if chunk == 0 and c == 0 and n == 0:
                        value = jnp.where(apart, value, 0.0)
                    high = value.astype(BF16)
                    coupling[chunk, number, 0, base, span] = high
                    coupling[chunk, number, 1, base, span] = (value - high.astype(F32)).astype(BF16)

    def contract(chunk, lefts):
        out = [None] * 3

        def add(a, value):
            out[a] = value if out[a] is None else out[a] + value

        def dot(left, number, part):
            return jnp.dot(left, coupling[chunk, number, part], preferred_element_type=F32)

        for number, (a, b) in enumerate(PAIRS):
            first, second = lefts[number]
            main, rest = dot(first, number, 0), dot(second, number, 1)
            add(a, main[:nfreq] + (main[nfreq:2 * nfreq] + rest[:nfreq]))
            if a != b:
                add(b, main[2 * nfreq:3 * nfreq] + (main[3 * nfreq:] + rest[nfreq:]))
        return out

    def apply(turn):
        with jax.named_scope("gather wait"):
            wait_for(gathered.at[turn], cols - 1, gather_recv.at[turn])
            if turn == 0:
                wait_for(sites, rows - 1, sites_recv)
        outs = [None] * tiles
        with jax.named_scope("contract"):
            if turn == 0:
                prepare()
            values = unpack(lambda s: gathered[turn, s], cols)
            highs = [value.astype(BF16).astype(F32) for value in values]
            lows = [value - high for value, high in zip(values, highs)]
            lefts = []
            for a, b in PAIRS:
                if a == b:
                    main, rest = [highs[a], lows[a]], [highs[a], lows[a]]
                else:
                    main, rest = [highs[b], lows[b], highs[a], lows[a]], [highs[b], highs[a]]
                lefts.append(tuple(jnp.concatenate(part, axis=0).astype(BF16) for part in (main, rest)))
            for chunk in range(tiles - 1, -1, -1):
                if turn == 0:
                    build(chunk)
                out = contract(chunk, lefts)
                outs[chunk] = out
                first = chunk * TILE
                for s in range(TILE):
                    cut = slice(s * piece, (s + 1) * piece)
                    block = jnp.concatenate([out[0][:, cut], out[1][:, cut], out[2][:, cut], zeros_tail], axis=1)
                    if first + s == 0:
                        landed[turn, 0] = block
                    else:
                        partial[turn, first + s] = block
                send_row(
                    lambda slot: partial.at[turn, slot], landed.at[turn], fold_send.at[turn], fold_recv.at[turn], 1,
                    range(first + TILE - 1, max(first - 1, 0), -1),
                )
        return outs

    def folded(turn):
        with jax.named_scope("fold wait"):
            wait_for(landed.at[turn], rows - 1, fold_recv.at[turn])
        return total_of([landed[turn, r] for r in range(rows)])

    def spread(turn, value):
        gathered[turn, 0] = value
        with jax.named_scope("gather send"):
            send_col(gathered.at[turn, 0], gathered.at[turn], gather_send.at[turn], gather_recv.at[turn])

    apply(0)
    powers = [source_full - folded(0)]
    scaled = []
    for turn in range(1, APPLICATIONS - 1):
        scaled.append(powers[-1] * inverse_diagonal)
        spread(turn, scaled[-1])
        apply(turn)
        powers.append(folded(turn))

    last = APPLICATIONS - 1
    scaled.append(powers[-1] * inverse_diagonal)
    spread(last, scaled[-1])
    mates[0] = scaled[-1]
    send_row(lambda slot: mates.at[0], mates, mates_send, mates_recv, -1)
    moments = jnp.zeros((nfreq, LANES), F32)
    for k, (i, j) in enumerate(MOMENTS):
        local = jnp.sum(scaled[i] * powers[j], axis=1, keepdims=True)
        moments = jnp.where(lane == k, local, moments)
    outs = apply(last)
    with jax.named_scope("mates wait"):
        wait_for(mates, rows - 1, mates_recv)
    terms = []
    for chunk in range(tiles):
        own = unpack(lambda s: mates[chunk * TILE + s], TILE)
        terms += [own[a] * outs[chunk][a] for a in range(3)]
    local = jnp.sum(total_of(terms), axis=1, keepdims=True)
    moments = jnp.where(lane == len(MOMENTS), local, moments)
    with jax.named_scope("sum"):
        col_sums[0] = moments
        send_col(col_sums.at[0], col_sums, sum_send.at[0], sum_recv.at[0])
        wait_for(col_sums, cols - 1, sum_recv.at[0])
        row_sums[0] = total_of([col_sums[c] for c in range(cols)])
        send_row(lambda slot: row_sums.at[0], row_sums, sum_send.at[1], sum_recv.at[1], -1)
        powers.append(folded(last))
        wait_for(row_sums, rows - 1, sum_recv.at[1])
    total = total_of([row_sums[r] for r in range(rows)])

    m = [jnp.broadcast_to(total[:, k:k + 1], (nfreq, LANES)) for k in range(6)]
    a0 = m[1] / m[0]
    h0 = m[0]
    h1 = m[2] - a0 * m[1]
    a1 = (m[3] - 2.0 * a0 * m[2] + a0 * a0 * m[1]) / h1
    b1 = h1 / h0
    c1 = -(a0 + a1)
    c0 = a0 * a1 - b1
    h2 = m[4] + c1 * m[3] + c0 * m[2]
    a2 = (m[5] + c1 * m[4] + c0 * m[3]) / h2 + c1
    b2 = h2 / h1
    e2 = c1 - a2
    e1 = c0 - a2 * c1 - b2
    e0 = b2 * a0 - a2 * c0
    top = 1.0 / (e2 - 1.0 - e1 + e0)
    p3, p2, p1, p0 = top, e2 * top, e1 * top, e0 * top
    s2 = -p3
    s1 = -p2 - s2
    s0 = -p1 - s1
    residual = p0 * powers[0] + p1 * powers[1] + p2 * powers[2] + p3 * powers[3]
    dipoles = start_full + (s0 * scaled[0] + s1 * scaled[1] + s2 * scaled[2])
    for a in range(3):
        dipoles_out[a] = dipoles[:, a * piece:(a + 1) * piece]
        residual_out[a] = residual[:, a * piece:(a + 1) * piece]

    for turn in range(APPLICATIONS):
        wait_for(gathered.at[turn], cols - 1, gather_send.at[turn])
        wait_for(landed.at[turn], rows - 1, fold_send.at[turn])
    wait_for(sites, rows - 1, sites_send)
    wait_for(mates, rows - 1, mates_send)
    wait_for(col_sums, cols - 1, sum_send.at[0])
    wait_for(row_sums, rows - 1, sum_send.at[1])


def solution(mesh):
    rows, cols = mesh.shape["row"], mesh.shape["col"]

    def shards(positions, atom_types, alpha_table, omega_table, radius_table, frequencies, field, start_dipoles):
        piece, nfreq = positions.shape[1], frequencies.shape[0]
        side = (10.0 * piece * rows * cols) ** (1.0 / 3.0)
        operands = (
            positions, atom_types.reshape(1, piece), alpha_table, omega_table, radius_table, frequencies,
            field, start_dipoles,
        )
        vmem = pl.BlockSpec(memory_space=pltpu.VMEM)
        tile = (nfreq, LANES)
        dma = pltpu.SemaphoreType.DMA
        places = [pltpu.VMEM] * 2 + [pltpu.SMEM] * 4 + [pltpu.VMEM] * 2
        return pl.pallas_call(
            functools.partial(kernel, rows, cols, piece, side),
            out_shape=(jax.ShapeDtypeStruct(field.shape, F32),) * 2,
            in_specs=[pl.BlockSpec(memory_space=pltpu.HBM)] * len(operands),
            out_specs=(vmem, vmem),
            scratch_shapes=[space(array.shape, array.dtype) for space, array in zip(places, operands)] + [
                pltpu.VMEM((APPLICATIONS, cols) + tile, F32),
                pltpu.VMEM((APPLICATIONS, rows) + tile, F32),
                pltpu.VMEM((APPLICATIONS, rows) + tile, F32),
                pltpu.VMEM((rows,) + tile, F32),
                pltpu.VMEM((rows,) + tile, F32),
                pltpu.VMEM((nfreq, rows * piece), F32),
                pltpu.VMEM((4, cols * piece, LANES), F32),
                pltpu.VMEM((rows // TILE, len(PAIRS), 2, cols * piece, TILE * piece), BF16),
                pltpu.VMEM((cols,) + tile, F32),
                pltpu.VMEM((rows,) + tile, F32),
                dma((len(operands),)),
                dma((APPLICATIONS,)), dma((APPLICATIONS,)),
                dma, dma,
                dma((APPLICATIONS,)), dma((APPLICATIONS,)),
                dma, dma,
                dma((2,)), dma((2,)),
            ],
            compiler_params=pltpu.CompilerParams(
                collective_id=0, has_side_effects=True, vmem_limit_bytes=64 * 1024 * 1024
            ),
        )(*operands)

    placed = (
        P(None, ("row", "col")),
        P(("row", "col")),
        P(),
        P(),
        P(),
        P(),
        P(None, None, ("row", "col")),
        P(None, None, ("row", "col")),
    )
    return jax.shard_map(
        shards,
        mesh=mesh,
        in_specs=placed,
        out_specs=(P(None, None, ("row", "col")), P(None, None, ("row", "col"))),
        check_vma=False,
    )
```

```python
import functools

import jax
import jax.numpy as jnp
from jax import lax
from jax.experimental import pallas as pl
from jax.experimental.pallas import tpu as pltpu
from jax.sharding import PartitionSpec as P

MESH = pl.DeviceIdType.MESH
F32, BF16 = jnp.float32, jnp.bfloat16
APPLICATIONS = 4
PAIRS = ((0, 0), (1, 1), (2, 2), (0, 1), (0, 2), (1, 2))
LANES = 128
TILE = 8
SHORT = 6
ROW_MINOR = 4
COL_MINOR = 2
MOMENTS = ((0, 0), (0, 1), (1, 1), (1, 2), (2, 2))


def pick(indices, table, count):
    value = jnp.full(indices.shape, table[0], F32)
    for number in range(1, count):
        value = jnp.where(indices == number, table[number], value)
    return value


def hops(step, length):
    return min(step, length - step)


def nearest_first(count, minor, hop_minor):
    major = count // minor
    offsets = [(far, near) for far in range(major) for near in range(minor)]
    return sorted(offsets, key=lambda o: (hops(o[0], major) + hop_minor * hops(o[1], minor), o))


def turned(me, count, minor):
    major = count // minor
    high, low = lax.div(me, minor), lax.rem(me, minor)
    highs = [lax.rem(high + step, major) * minor for step in range(major)]
    lows = [lax.rem(low + step, minor) for step in range(minor)]
    return highs, lows


def kernel(
    rows, cols, piece, side,
    positions_hbm, types_hbm, alphas_hbm, omegas_hbm, radii_hbm, frequencies_hbm, field_hbm, start_hbm,
    out_ref,
    positions, types, alphas, omegas, radii, frequencies, field, start,
    gathered, partial, landed, sites, mates, own_sites, columns, coupling, col_sums, row_sums,
    load_sem, gather_send, gather_recv, sites_send, sites_recv, fold_send, fold_recv,
    mates_send, mates_recv, sum_send, sum_recv,
):
    nfreq, ntypes = frequencies.shape[0], alphas.shape[0]
    row, col = lax.axis_index("row"), lax.axis_index("col")
    tiles = rows // TILE
    group = LANES // piece
    depth = TILE * piece

    loads = [
        pltpu.make_async_copy(source, target, load_sem.at[number])
        for number, (source, target) in enumerate((
            (positions_hbm, positions), (types_hbm, types), (alphas_hbm, alphas), (omegas_hbm, omegas),
            (radii_hbm, radii), (frequencies_hbm, frequencies), (field_hbm, field), (start_hbm, start),
        ))
    ]
    barrier = pltpu.get_barrier_semaphore()

    row_offsets = nearest_first(rows, ROW_MINOR, 1)
    col_offsets = nearest_first(cols, COL_MINOR, 0.5)
    row_high, row_low = turned(row, rows, ROW_MINOR)
    col_high, col_low = turned(col, cols, COL_MINOR)

    def row_peer(slot, sign):
        far, near = row_offsets[slot]
        return (row_high[sign * far % len(row_high)] + row_low[sign * near % len(row_low)], col)

    def col_peer(slot, sign):
        far, near = col_offsets[slot]
        return (row, col_high[sign * far % len(col_high)] + col_low[sign * near % len(col_low)])

    row_order = range(rows - 1, 0, -1)
    col_order = range(cols - 1, 0, -1)

    with jax.named_scope("greet"):
        for slot in row_order:
            pl.semaphore_signal(barrier, inc=1, device_id=row_peer(slot, 1), device_id_type=MESH)
        for slot in col_order:
            pl.semaphore_signal(barrier, inc=1, device_id=col_peer(slot, 1), device_id_type=MESH)

    for load in loads:
        load.start()

    def send_row(source_of, target, send_sem, recv_sem, sign, slots=row_order, height=None):
        for slot in slots:
            pltpu.make_async_remote_copy(
                src_ref=source_of(slot), dst_ref=target.at[slot] if height is None else target.at[slot, pl.ds(0, height)],
                send_sem=send_sem, recv_sem=recv_sem,
                device_id=row_peer(slot, sign), device_id_type=MESH,
            ).start()

    def send_col(source, target, send_sem, recv_sem):
        for slot in col_order:
            pltpu.make_async_remote_copy(
                src_ref=source, dst_ref=target.at[slot], send_sem=send_sem, recv_sem=recv_sem,
                device_id=col_peer(slot, -1), device_id_type=MESH,
            ).start()

    def wait_for(buffer, count, sem, height=None):
        view = buffer.at[pl.ds(0, count)] if height is None else buffer.at[pl.ds(0, count), pl.ds(0, height)]
        pltpu.make_async_copy(view, view, sem).wait()

    def packed(ref):
        return jnp.concatenate([ref[0], ref[1], ref[2]], axis=1)

    with jax.named_scope("load"):
        for load in loads:
            load.wait()
    lane = lax.broadcasted_iota(jnp.int32, (nfreq, LANES), 1)
    level = lax.broadcasted_iota(jnp.int32, (nfreq, LANES), 0)
    kinds = types[...]
    radius = pick(kinds, radii, ntypes)
    place = positions[...] * side
    pad = jnp.zeros((nfreq - 4, piece), F32)
    site = jnp.concatenate([place, radius, pad], axis=0)
    start_packed = packed(start)
    message = jnp.concatenate([start_packed, site], axis=1)
    gathered[0, 0] = message
    sites[0] = message
    with jax.named_scope("barrier"):
        pl.semaphore_wait(barrier, rows + cols - 2)
    with jax.named_scope("first send"):
        send_row(lambda slot: sites.at[0], sites, sites_send, sites_recv, -1)
        send_col(gathered.at[0, 0], gathered.at[0], gather_send.at[0], gather_recv.at[0])

    kinds_packed = jnp.broadcast_to(jnp.concatenate([kinds] * group, axis=1), (nfreq, LANES))
    omega = pick(kinds_packed, omegas, ntypes)
    alpha = pick(kinds_packed, alphas, ntypes)
    ratio = pick(level, frequencies, nfreq) / omega
    diagonal = (1.0 + ratio * ratio) / alpha
    inverse_diagonal = alpha / (1.0 + ratio * ratio)
    zeros_tail = jnp.zeros((nfreq, LANES - 3 * piece), F32)
    start_full = jnp.concatenate([start_packed, zeros_tail], axis=1)
    field_full = jnp.concatenate([packed(field), zeros_tail], axis=1)
    source_full = field_full - diagonal * start_full

    def total_of(values):
        while len(values) > 1:
            values = [sum(values[k:k + 2]) for k in range(0, len(values), 2)]
        return values[0]

    def unpack(block_of, count):
        blocks = [block_of(s) for s in range(count)]
        return [
            jnp.concatenate(
                [
                    jnp.concatenate([blocks[t + q][:, a * piece:(a + 1) * piece] for q in range(group)], axis=1)
                    for t in range(0, count, group)
                ],
                axis=1,
            )
            for a in range(3)
        ]

    def prepare():
        for c in range(cols):
            across = gathered[0, c].T[3 * piece:, :]
            for q in range(4):
                columns[q, c * piece:(c + 1) * piece, :] = jnp.broadcast_to(across[:, q:q + 1], (piece, LANES))
        for r in range(rows):
            own_sites[:, r * piece:(r + 1) * piece] = sites[r][:, 3 * piece:]

    apart = (
        lax.broadcasted_iota(jnp.int32, (piece, LANES), 0) != lax.broadcasted_iota(jnp.int32, (piece, LANES), 1)
    )

    def build(chunk):
        for c in range(cols):
            base = slice(c * piece, (c + 1) * piece)
            column = [columns[q, base, :] for q in range(4)]
            for n in range(depth // LANES):
                span = slice(n * LANES, (n + 1) * LANES)
                place = slice(chunk * depth + n * LANES, chunk * depth + (n + 1) * LANES)
                offset = [column[q] - own_sites[q:q + 1, place] for q in range(3)]
                reach = column[3] + own_sites[3:4, place]
                square = offset[0] * offset[0] + offset[1] * offset[1] + offset[2] * offset[2] + reach * reach
                inverse = lax.rsqrt(square)
                second = inverse * inverse
                cube = second * inverse
                fifth = -3.0 * (cube * second)
                weighted = [offset[q] * fifth for q in range(3)]
                for number, (a, b) in enumerate(PAIRS):
                    value = weighted[a] * offset[b]
                    if a == b:
                        value = value + cube
                    if chunk == 0 and c == 0 and n == 0:
                        value = jnp.where(apart, value, 0.0)
                    high = value.astype(BF16)
                    coupling[chunk, number, 0, base, span] = high
                    coupling[chunk, number, 1, base, span] = (value - high.astype(F32)).astype(BF16)

    def contract(chunk, lefts):
        out = [None] * 3

        def add(a, value):
            out[a] = value if out[a] is None else out[a] + value

        def dot(left, number, part):
            return jnp.dot(left, coupling[chunk, number, part], preferred_element_type=F32)

        for number, (a, b) in enumerate(PAIRS):
            first, second = lefts[number]
            main, rest = dot(first, number, 0), dot(second, number, 1)
            add(a, main[:nfreq] + (main[nfreq:2 * nfreq] + rest[:nfreq]))
            if a != b:
                add(b, main[2 * nfreq:3 * nfreq] + (main[3 * nfreq:] + rest[nfreq:]))
        return out

    def apply(turn):
        with jax.named_scope("gather wait"):
            wait_for(gathered.at[turn], cols - 1, gather_recv.at[turn])
            if turn == 0:
                wait_for(sites, rows - 1, sites_recv)
        outs = [None] * tiles
        with jax.named_scope("contract"):
            if turn == 0:
                prepare()
            values = unpack(lambda s: gathered[turn, s], cols)
            highs = [value.astype(BF16).astype(F32) for value in values]
            lows = [value - high for value, high in zip(values, highs)]
            lefts = []
            for a, b in PAIRS:
                if a == b:
                    main, rest = [highs[a], lows[a]], [highs[a], lows[a]]
                else:
                    main, rest = [highs[b], lows[b], highs[a], lows[a]], [highs[b], highs[a]]
                lefts.append(tuple(jnp.concatenate(part, axis=0).astype(BF16) for part in (main, rest)))
            for chunk in range(tiles - 1, -1, -1):
                if turn == 0:
                    build(chunk)
                out = contract(chunk, lefts)
                outs[chunk] = out
                first = chunk * TILE
                low = jnp.concatenate([out[a][SHORT:] for a in range(3)] + [out[0][SHORT:]], axis=0)
                for s in range(TILE):
                    cut = slice(s * piece, (s + 1) * piece)
                    block = jnp.concatenate([out[0][:, cut], out[1][:, cut], out[2][:, cut], low[:, cut]], axis=1)
                    if first + s == 0:
                        landed[turn, 0] = block
                    else:
                        partial[turn, first + s] = block
                send_row(
                    lambda slot: partial.at[turn, slot, pl.ds(0, SHORT)], landed.at[turn], fold_send.at[turn],
                    fold_recv.at[turn], 1, range(first + TILE - 1, max(first - 1, 0), -1), SHORT,
                )
        return outs

    def folded(turn):
        with jax.named_scope("fold wait"):
            wait_for(landed.at[turn], rows - 1, fold_recv.at[turn], SHORT)
        total = total_of([landed[turn, r, :SHORT] for r in range(rows)])
        parts = [
            jnp.concatenate(
                [total[:, a * piece:(a + 1) * piece], total[a * (nfreq - SHORT):(a + 1) * (nfreq - SHORT), 3 * piece:]], axis=0
            )
            for a in range(3)
        ]
        return jnp.concatenate(parts + [zeros_tail], axis=1)

    def spread(turn, value):
        gathered[turn, 0] = value
        with jax.named_scope("gather send"):
            send_col(gathered.at[turn, 0], gathered.at[turn], gather_send.at[turn], gather_recv.at[turn])

    apply(0)
    powers = [source_full - folded(0)]
    scaled = []
    for turn in range(1, APPLICATIONS - 1):
        scaled.append(powers[-1] * inverse_diagonal)
        spread(turn, scaled[-1])
        apply(turn)
        powers.append(folded(turn))

    last = APPLICATIONS - 1
    scaled.append(powers[-1] * inverse_diagonal)
    spread(last, scaled[-1])
    mates[0] = scaled[-1]
    send_row(lambda slot: mates.at[0], mates, mates_send, mates_recv, -1)
    moments = jnp.zeros((nfreq, LANES), F32)
    for k, (i, j) in enumerate(MOMENTS):
        local = jnp.sum(scaled[i] * powers[j], axis=1, keepdims=True)
        moments = jnp.where(lane == k, local, moments)
    outs = apply(last)
    with jax.named_scope("mates wait"):
        wait_for(mates, rows - 1, mates_recv)
    terms = []
    for chunk in range(tiles):
        own = unpack(lambda s: mates[chunk * TILE + s], TILE)
        terms += [own[a] * outs[chunk][a] for a in range(3)]
    local = jnp.sum(total_of(terms), axis=1, keepdims=True)
    moments = jnp.where(lane == len(MOMENTS), local, moments)
    with jax.named_scope("sum"):
        spaced = pltpu.roll(moments, 0, 1, stride=LANES // nfreq, stride_axis=0)
        col_sums[0] = jnp.sum(spaced, axis=0, keepdims=True)
        send_col(col_sums.at[0], col_sums, sum_send.at[0], sum_recv.at[0])
        wait_for(col_sums, cols - 1, sum_recv.at[0])
        row_sums[0] = total_of([col_sums[c] for c in range(cols)])
        send_row(lambda slot: row_sums.at[0], row_sums, sum_send.at[1], sum_recv.at[1], -1)
        powers.append(folded(last))
        wait_for(row_sums, rows - 1, sum_recv.at[1])
    total = jnp.broadcast_to(total_of([row_sums[r] for r in range(rows)]), (nfreq, LANES))
    column_of = lane - level * (LANES // nfreq)

    m = [jnp.sum(jnp.where(column_of == k, total, 0.0), axis=1, keepdims=True) for k in range(len(MOMENTS) + 1)]
    a0 = m[1] / m[0]
    h0 = m[0]
    h1 = m[2] - a0 * m[1]
    a1 = (m[3] - 2.0 * a0 * m[2] + a0 * a0 * m[1]) / h1
    b1 = h1 / h0
    c1 = -(a0 + a1)
    c0 = a0 * a1 - b1
    h2 = m[4] + c1 * m[3] + c0 * m[2]
    a2 = (m[5] + c1 * m[4] + c0 * m[3]) / h2 + c1
    b2 = h2 / h1
    e2 = c1 - a2
    e1 = c0 - a2 * c1 - b2
    e0 = b2 * a0 - a2 * c0
    top = 1.0 / (e2 - 1.0 - e1 + e0)
    p3, p2, p1, p0 = top, e2 * top, e1 * top, e0 * top
    s2 = -p3
    s1 = -p2 - s2
    s0 = -p1 - s1
    residual = p0 * powers[0] + p1 * powers[1] + p2 * powers[2] + p3 * powers[3]
    dipoles = start_full + (s0 * scaled[0] + s1 * scaled[1] + s2 * scaled[2])
    for a in range(3):
        out_ref[0, a] = dipoles[:, a * piece:(a + 1) * piece]
        out_ref[1, a] = residual[:, a * piece:(a + 1) * piece]

    for turn in range(APPLICATIONS):
        wait_for(gathered.at[turn], cols - 1, gather_send.at[turn])
        wait_for(landed.at[turn], rows - 1, fold_send.at[turn], SHORT)
    wait_for(sites, rows - 1, sites_send)
    wait_for(mates, rows - 1, mates_send)
    wait_for(col_sums, cols - 1, sum_send.at[0])
    wait_for(row_sums, rows - 1, sum_send.at[1])


def solution(mesh):
    rows, cols = mesh.shape["row"], mesh.shape["col"]

    def shards(positions, atom_types, alpha_table, omega_table, radius_table, frequencies, field, start_dipoles):
        piece, nfreq = positions.shape[1], frequencies.shape[0]
        side = (10.0 * piece * rows * cols) ** (1.0 / 3.0)
        operands = (
            positions, atom_types.reshape(1, piece), alpha_table, omega_table, radius_table, frequencies,
            field, start_dipoles,
        )
        vmem = pl.BlockSpec(memory_space=pltpu.VMEM)
        tile = (nfreq, LANES)
        dma = pltpu.SemaphoreType.DMA
        places = [pltpu.VMEM] * 2 + [pltpu.SMEM] * 4 + [pltpu.VMEM] * 2
        both = pl.pallas_call(
            functools.partial(kernel, rows, cols, piece, side),
            out_shape=jax.ShapeDtypeStruct((2,) + field.shape, F32),
            in_specs=[pl.BlockSpec(memory_space=pltpu.HBM)] * len(operands),
            out_specs=vmem,
            scratch_shapes=[space(array.shape, array.dtype) for space, array in zip(places, operands)] + [
                pltpu.VMEM((APPLICATIONS, cols) + tile, F32),
                pltpu.VMEM((APPLICATIONS, rows) + tile, F32),
                pltpu.VMEM((APPLICATIONS, rows) + tile, F32),
                pltpu.VMEM((rows,) + tile, F32),
                pltpu.VMEM((rows,) + tile, F32),
                pltpu.VMEM((nfreq, rows * piece), F32),
                pltpu.VMEM((4, cols * piece, LANES), F32),
                pltpu.VMEM((rows // TILE, len(PAIRS), 2, cols * piece, TILE * piece), BF16),
                pltpu.VMEM((cols, 1, LANES), F32),
                pltpu.VMEM((rows, 1, LANES), F32),
                dma((len(operands),)),
                dma((APPLICATIONS,)), dma((APPLICATIONS,)),
                dma, dma,
                dma((APPLICATIONS,)), dma((APPLICATIONS,)),
                dma, dma,
                dma((2,)), dma((2,)),
            ],
            compiler_params=pltpu.CompilerParams(
                collective_id=0, has_side_effects=True, vmem_limit_bytes=64 * 1024 * 1024
            ),
        )(*operands)
        return both[0], both[1]

    placed = (
        P(None, ("row", "col")),
        P(("row", "col")),
        P(),
        P(),
        P(),
        P(),
        P(None, None, ("row", "col")),
        P(None, None, ("row", "col")),
    )
    return jax.shard_map(
        shards,
        mesh=mesh,
        in_specs=placed,
        out_specs=(P(None, None, ("row", "col")), P(None, None, ("row", "col"))),
        check_vma=False,
    )
```

```python
import functools

import jax
import jax.numpy as jnp
from jax import lax
from jax.experimental import pallas as pl
from jax.experimental.pallas import tpu as pltpu
from jax.sharding import PartitionSpec as P

MESH = pl.DeviceIdType.MESH
F32, BF16 = jnp.float32, jnp.bfloat16
APPLICATIONS = 4
PAIRS = ((0, 0), (1, 1), (2, 2), (0, 1), (0, 2), (1, 2))
LANES = 128
TILE = 8
SHORT = 6
ROW_MINOR = 4
COL_MINOR = 2
COL_FIRST = 1
MOMENTS = ((0, 0), (0, 1), (1, 1), (1, 2), (2, 2))


def pick(indices, table, count):
    value = jnp.full(indices.shape, table[0], F32)
    for number in range(1, count):
        value = jnp.where(indices == number, table[number], value)
    return value


def hops(step, length):
    return min(step, length - step)


def nearest_first(count, minor, hop_minor):
    major = count // minor
    offsets = [(far, near) for far in range(major) for near in range(minor)]
    return sorted(offsets, key=lambda o: (hops(o[0], major) + hop_minor * hops(o[1], minor), o))


def turned(me, count, minor):
    major = count // minor
    high, low = lax.div(me, minor), lax.rem(me, minor)
    highs = [lax.rem(high + step, major) * minor for step in range(major)]
    lows = [lax.rem(low + step, minor) for step in range(minor)]
    return highs, lows


def kernel(
    rows, cols, piece, side,
    positions_hbm, types_hbm, alphas_hbm, omegas_hbm, radii_hbm, frequencies_hbm, field_hbm, start_hbm,
    out_ref,
    positions, types, alphas, omegas, radii, frequencies, field, start,
    gathered, partial, landed, sites, mates, own_sites, columns, coupling, col_sums, row_sums,
    load_sem, gather_send, gather_recv, sites_send, sites_recv, fold_send, fold_recv,
    mates_send, mates_recv, sum_send, sum_recv,
):
    nfreq, ntypes = frequencies.shape[0], alphas.shape[0]
    row, col = lax.axis_index("row"), lax.axis_index("col")
    tiles = rows // TILE
    group = LANES // piece
    depth = TILE * piece

    loads = [
        pltpu.make_async_copy(source, target, load_sem.at[number])
        for number, (source, target) in enumerate((
            (positions_hbm, positions), (types_hbm, types), (alphas_hbm, alphas), (omegas_hbm, omegas),
            (radii_hbm, radii), (frequencies_hbm, frequencies), (field_hbm, field), (start_hbm, start),
        ))
    ]
    barrier = pltpu.get_barrier_semaphore()

    row_offsets = nearest_first(rows, ROW_MINOR, 1)
    col_offsets = nearest_first(cols, COL_MINOR, 0.5)
    row_high, row_low = turned(row, rows, ROW_MINOR)
    col_high, col_low = turned(col, cols, COL_MINOR)

    def row_peer(slot, sign):
        far, near = row_offsets[slot]
        return (row_high[sign * far % len(row_high)] + row_low[sign * near % len(row_low)], col)

    def col_peer(slot, sign):
        far, near = col_offsets[slot]
        return (row, col_high[sign * far % len(col_high)] + col_low[sign * near % len(col_low)])

    row_order = range(rows - 1, 0, -1)
    col_order = range(cols - 1, 0, -1)

    reach_row = [hops(far, len(row_high)) + hops(near, len(row_low)) for far, near in row_offsets]
    reach_col = [hops(far, len(col_high)) for far, _ in col_offsets]
    everyone = sorted(
        [(-reach_row[slot], False, -slot) for slot in row_order]
        + [(-reach_col[slot] - COL_FIRST, True, -slot) for slot in col_order]
    )

    with jax.named_scope("greet"):
        for _, along_col, slot in everyone:
            peer = col_peer(-slot, 1) if along_col else row_peer(-slot, 1)
            pl.semaphore_signal(barrier, inc=1, device_id=peer, device_id_type=MESH)

    for load in loads:
        load.start()

    def send_row(source_of, target, send_sem, recv_sem, sign, slots=row_order, height=None):
        for slot in slots:
            pltpu.make_async_remote_copy(
                src_ref=source_of(slot), dst_ref=target.at[slot] if height is None else target.at[slot, pl.ds(0, height)],
                send_sem=send_sem, recv_sem=recv_sem,
                device_id=row_peer(slot, sign), device_id_type=MESH,
            ).start()

    def send_col(source, target, send_sem, recv_sem, slots=col_order):
        for slot in slots:
            pltpu.make_async_remote_copy(
                src_ref=source, dst_ref=target.at[slot], send_sem=send_sem, recv_sem=recv_sem,
                device_id=col_peer(slot, -1), device_id_type=MESH,
            ).start()

    def wait_for(buffer, count, sem, height=None):
        view = buffer.at[pl.ds(0, count)] if height is None else buffer.at[pl.ds(0, count), pl.ds(0, height)]
        pltpu.make_async_copy(view, view, sem).wait()

    def packed(ref):
        return jnp.concatenate([ref[0], ref[1], ref[2]], axis=1)

    with jax.named_scope("load"):
        for load in loads:
            load.wait()
    lane = lax.broadcasted_iota(jnp.int32, (nfreq, LANES), 1)
    level = lax.broadcasted_iota(jnp.int32, (nfreq, LANES), 0)
    kinds = types[...]
    radius = pick(kinds, radii, ntypes)
    place = positions[...] * side
    pad = jnp.zeros((nfreq - 4, piece), F32)
    site = jnp.concatenate([place, radius, pad], axis=0)
    start_packed = packed(start)
    message = jnp.concatenate([start_packed, site], axis=1)
    gathered[0, 0] = message
    sites[0] = message
    with jax.named_scope("barrier"):
        pl.semaphore_wait(barrier, rows + cols - 2)
    with jax.named_scope("first send"):
        for _, along_col, slot in everyone:
            if along_col:
                send_col(gathered.at[0, 0], gathered.at[0], gather_send.at[0], gather_recv.at[0], (-slot,))
            else:
                send_row(lambda _: sites.at[0, pl.ds(0, 4)], sites, sites_send, sites_recv, -1, (-slot,), 4)

    kinds_packed = jnp.broadcast_to(jnp.concatenate([kinds] * group, axis=1), (nfreq, LANES))
    omega = pick(kinds_packed, omegas, ntypes)
    alpha = pick(kinds_packed, alphas, ntypes)
    ratio = pick(level, frequencies, nfreq) / omega
    diagonal = (1.0 + ratio * ratio) / alpha
    inverse_diagonal = alpha / (1.0 + ratio * ratio)
    zeros_tail = jnp.zeros((nfreq, LANES - 3 * piece), F32)
    start_full = jnp.concatenate([start_packed, zeros_tail], axis=1)
    field_full = jnp.concatenate([packed(field), zeros_tail], axis=1)
    source_full = field_full - diagonal * start_full

    def total_of(values):
        while len(values) > 1:
            values = [sum(values[k:k + 2]) for k in range(0, len(values), 2)]
        return values[0]

    def unpack(block_of, count):
        blocks = [block_of(s) for s in range(count)]
        return [
            jnp.concatenate(
                [
                    jnp.concatenate([blocks[t + q][:, a * piece:(a + 1) * piece] for q in range(group)], axis=1)
                    for t in range(0, count, group)
                ],
                axis=1,
            )
            for a in range(3)
        ]

    def prepare():
        for c in range(cols):
            across = gathered[0, c].T[3 * piece:, :]
            for q in range(4):
                columns[q, c * piece:(c + 1) * piece, :] = jnp.broadcast_to(across[:, q:q + 1], (piece, LANES))

    def place_sites():
        for r in range(rows):
            own_sites[:, r * piece:(r + 1) * piece] = sites[r, :4, 3 * piece:]

    apart = (
        lax.broadcasted_iota(jnp.int32, (piece, LANES), 0) != lax.broadcasted_iota(jnp.int32, (piece, LANES), 1)
    )

    def build(chunk):
        for c in range(cols):
            base = slice(c * piece, (c + 1) * piece)
            column = [columns[q, base, :] for q in range(4)]
            for n in range(depth // LANES):
                span = slice(n * LANES, (n + 1) * LANES)
                place = slice(chunk * depth + n * LANES, chunk * depth + (n + 1) * LANES)
                offset = [column[q] - own_sites[q:q + 1, place] for q in range(3)]
                reach = column[3] + own_sites[3:4, place]
                square = offset[0] * offset[0] + offset[1] * offset[1] + offset[2] * offset[2] + reach * reach
                inverse = lax.rsqrt(square)
                second = inverse * inverse
                cube = second * inverse
                fifth = -3.0 * (cube * second)
                weighted = [offset[q] * fifth for q in range(3)]
                for number, (a, b) in enumerate(PAIRS):
                    value = weighted[a] * offset[b]
                    if a == b:
                        value = value + cube
                    if chunk == 0 and c == 0 and n == 0:
                        value = jnp.where(apart, value, 0.0)
                    high = value.astype(BF16)
                    coupling[chunk, number, 0, base, span] = high
                    coupling[chunk, number, 1, base, span] = (value - high.astype(F32)).astype(BF16)

    def contract(chunk, lefts):
        out = [None] * 3

        def add(a, value):
            out[a] = value if out[a] is None else out[a] + value

        def dot(left, number, part):
            return jnp.dot(left, coupling[chunk, number, part], preferred_element_type=F32)

        for number, (a, b) in enumerate(PAIRS):
            first, second = lefts[number]
            main, rest = dot(first, number, 0), dot(second, number, 1)
            add(a, main[:nfreq] + (main[nfreq:2 * nfreq] + rest[:nfreq]))
            if a != b:
                add(b, main[2 * nfreq:3 * nfreq] + (main[3 * nfreq:] + rest[nfreq:]))
        return out

    def apply(turn):
        with jax.named_scope("gather wait"):
            wait_for(gathered.at[turn], cols - 1, gather_recv.at[turn])
        if turn == 0:
            prepare()
            with jax.named_scope("sites wait"):
                wait_for(sites, rows - 1, sites_recv, 4)
            place_sites()
        outs = [None] * tiles
        with jax.named_scope("contract"):
            values = unpack(lambda s: gathered[turn, s], cols)
            highs = [value.astype(BF16).astype(F32) for value in values]
            lows = [value - high for value, high in zip(values, highs)]
            lefts = []
            for a, b in PAIRS:
                if a == b:
                    main, rest = [highs[a], lows[a]], [highs[a], lows[a]]
                else:
                    main, rest = [highs[b], lows[b], highs[a], lows[a]], [highs[b], highs[a]]
                lefts.append(tuple(jnp.concatenate(part, axis=0).astype(BF16) for part in (main, rest)))
            for chunk in range(tiles - 1, -1, -1):
                if turn == 0:
                    build(chunk)
                out = contract(chunk, lefts)
                outs[chunk] = out
                first = chunk * TILE
                low = jnp.concatenate([out[a][SHORT:] for a in range(3)] + [out[0][SHORT:]], axis=0)
                for s in range(TILE):
                    cut = slice(s * piece, (s + 1) * piece)
                    block = jnp.concatenate([out[0][:, cut], out[1][:, cut], out[2][:, cut], low[:, cut]], axis=1)
                    if first + s == 0:
                        landed[turn, 0] = block
                    else:
                        partial[turn, first + s] = block
                send_row(
                    lambda slot: partial.at[turn, slot, pl.ds(0, SHORT)], landed.at[turn], fold_send.at[turn],
                    fold_recv.at[turn], 1, range(first + TILE - 1, max(first - 1, 0), -1), SHORT,
                )
        return outs

    def folded(turn):
        with jax.named_scope("fold wait"):
            wait_for(landed.at[turn], rows - 1, fold_recv.at[turn], SHORT)
        total = total_of([landed[turn, r, :SHORT] for r in range(rows)])
        parts = [
            jnp.concatenate(
                [total[:, a * piece:(a + 1) * piece], total[a * (nfreq - SHORT):(a + 1) * (nfreq - SHORT), 3 * piece:]], axis=0
            )
            for a in range(3)
        ]
        return jnp.concatenate(parts + [zeros_tail], axis=1)

    def spread(turn, value):
        gathered[turn, 0] = value
        with jax.named_scope("gather send"):
            send_col(gathered.at[turn, 0], gathered.at[turn], gather_send.at[turn], gather_recv.at[turn])

    apply(0)
    powers = [source_full - folded(0)]
    scaled = []
    for turn in range(1, APPLICATIONS - 1):
        scaled.append(powers[-1] * inverse_diagonal)
        spread(turn, scaled[-1])
        apply(turn)
        powers.append(folded(turn))

    last = APPLICATIONS - 1
    scaled.append(powers[-1] * inverse_diagonal)
    spread(last, scaled[-1])
    mates[0] = scaled[-1]
    send_row(lambda slot: mates.at[0], mates, mates_send, mates_recv, -1)
    moments = jnp.zeros((nfreq, LANES), F32)
    for k, (i, j) in enumerate(MOMENTS):
        local = jnp.sum(scaled[i] * powers[j], axis=1, keepdims=True)
        moments = jnp.where(lane == k, local, moments)
    outs = apply(last)
    with jax.named_scope("mates wait"):
        wait_for(mates, rows - 1, mates_recv)
    terms = []
    for chunk in range(tiles):
        own = unpack(lambda s: mates[chunk * TILE + s], TILE)
        terms += [own[a] * outs[chunk][a] for a in range(3)]
    local = jnp.sum(total_of(terms), axis=1, keepdims=True)
    moments = jnp.where(lane == len(MOMENTS), local, moments)
    with jax.named_scope("sum"):
        spaced = pltpu.roll(moments, 0, 1, stride=LANES // nfreq, stride_axis=0)
        col_sums[0] = jnp.sum(spaced, axis=0, keepdims=True)
        send_col(col_sums.at[0], col_sums, sum_send.at[0], sum_recv.at[0])
        wait_for(col_sums, cols - 1, sum_recv.at[0])
        row_sums[0] = total_of([col_sums[c] for c in range(cols)])
        send_row(lambda slot: row_sums.at[0], row_sums, sum_send.at[1], sum_recv.at[1], -1)
        powers.append(folded(last))
        wait_for(row_sums, rows - 1, sum_recv.at[1])
    total = jnp.broadcast_to(total_of([row_sums[r] for r in range(rows)]), (nfreq, LANES))
    column_of = lane - level * (LANES // nfreq)

    m = [jnp.sum(jnp.where(column_of == k, total, 0.0), axis=1, keepdims=True) for k in range(len(MOMENTS) + 1)]
    a0 = m[1] / m[0]
    h0 = m[0]
    h1 = m[2] - a0 * m[1]
    a1 = (m[3] - 2.0 * a0 * m[2] + a0 * a0 * m[1]) / h1
    b1 = h1 / h0
    c1 = -(a0 + a1)
    c0 = a0 * a1 - b1
    h2 = m[4] + c1 * m[3] + c0 * m[2]
    a2 = (m[5] + c1 * m[4] + c0 * m[3]) / h2 + c1
    b2 = h2 / h1
    e2 = c1 - a2
    e1 = c0 - a2 * c1 - b2
    e0 = b2 * a0 - a2 * c0
    top = 1.0 / (e2 - 1.0 - e1 + e0)
    p3, p2, p1, p0 = top, e2 * top, e1 * top, e0 * top
    s2 = -p3
    s1 = -p2 - s2
    s0 = -p1 - s1
    residual = p0 * powers[0] + p1 * powers[1] + p2 * powers[2] + p3 * powers[3]
    dipoles = start_full + (s0 * scaled[0] + s1 * scaled[1] + s2 * scaled[2])
    for a in range(3):
        out_ref[0, a] = dipoles[:, a * piece:(a + 1) * piece]
        out_ref[1, a] = residual[:, a * piece:(a + 1) * piece]

    for turn in range(APPLICATIONS):
        wait_for(gathered.at[turn], cols - 1, gather_send.at[turn])
        wait_for(landed.at[turn], rows - 1, fold_send.at[turn], SHORT)
    wait_for(sites, rows - 1, sites_send, 4)
    wait_for(mates, rows - 1, mates_send)
    wait_for(col_sums, cols - 1, sum_send.at[0])
    wait_for(row_sums, rows - 1, sum_send.at[1])


def solution(mesh):
    rows, cols = mesh.shape["row"], mesh.shape["col"]

    def shards(positions, atom_types, alpha_table, omega_table, radius_table, frequencies, field, start_dipoles):
        piece, nfreq = positions.shape[1], frequencies.shape[0]
        side = (10.0 * piece * rows * cols) ** (1.0 / 3.0)
        operands = (
            positions, atom_types.reshape(1, piece), alpha_table, omega_table, radius_table, frequencies,
            field, start_dipoles,
        )
        vmem = pl.BlockSpec(memory_space=pltpu.VMEM)
        tile = (nfreq, LANES)
        dma = pltpu.SemaphoreType.DMA
        places = [pltpu.VMEM] * 2 + [pltpu.SMEM] * 4 + [pltpu.VMEM] * 2
        both = pl.pallas_call(
            functools.partial(kernel, rows, cols, piece, side),
            out_shape=jax.ShapeDtypeStruct((2,) + field.shape, F32),
            in_specs=[pl.BlockSpec(memory_space=pltpu.HBM)] * len(operands),
            out_specs=vmem,
            scratch_shapes=[space(array.shape, array.dtype) for space, array in zip(places, operands)] + [
                pltpu.VMEM((APPLICATIONS, cols) + tile, F32),
                pltpu.VMEM((APPLICATIONS, rows) + tile, F32),
                pltpu.VMEM((APPLICATIONS, rows) + tile, F32),
                pltpu.VMEM((rows,) + tile, F32),
                pltpu.VMEM((rows,) + tile, F32),
                pltpu.VMEM((4, rows * piece), F32),
                pltpu.VMEM((4, cols * piece, LANES), F32),
                pltpu.VMEM((rows // TILE, len(PAIRS), 2, cols * piece, TILE * piece), BF16),
                pltpu.VMEM((cols, 1, LANES), F32),
                pltpu.VMEM((rows, 1, LANES), F32),
                dma((len(operands),)),
                dma((APPLICATIONS,)), dma((APPLICATIONS,)),
                dma, dma,
                dma((APPLICATIONS,)), dma((APPLICATIONS,)),
                dma, dma,
                dma((2,)), dma((2,)),
            ],
            compiler_params=pltpu.CompilerParams(
                collective_id=0, has_side_effects=True, vmem_limit_bytes=64 * 1024 * 1024
            ),
        )(*operands)
        return both[0], both[1]

    placed = (
        P(None, ("row", "col")),
        P(("row", "col")),
        P(),
        P(),
        P(),
        P(),
        P(None, None, ("row", "col")),
        P(None, None, ("row", "col")),
    )
    return jax.shard_map(
        shards,
        mesh=mesh,
        in_specs=placed,
        out_specs=(P(None, None, ("row", "col")), P(None, None, ("row", "col"))),
        check_vma=False,
    )
```

```python
import functools

import jax
import jax.numpy as jnp
from jax import lax
from jax.experimental import pallas as pl
from jax.experimental.pallas import tpu as pltpu
from jax.sharding import PartitionSpec as P

MESH = pl.DeviceIdType.MESH
F32, BF16 = jnp.float32, jnp.bfloat16
APPLICATIONS = 4
PAIRS = ((0, 0), (1, 1), (2, 2), (0, 1), (0, 2), (1, 2))
LANES = 128
TILE = 8
SHORT = 6
ROW_MINOR = 4
COL_MINOR = 2
COL_FIRST = 1
MOMENTS = ((0, 0), (0, 1), (1, 1), (1, 2), (2, 2))


def pick(indices, table, count):
    value = jnp.full(indices.shape, table[0], F32)
    for number in range(1, count):
        value = jnp.where(indices == number, table[number], value)
    return value


def hops(step, length):
    return min(step, length - step)


def nearest_first(count, minor, hop_minor):
    major = count // minor
    offsets = [(far, near) for far in range(major) for near in range(minor)]
    return sorted(offsets, key=lambda o: (hops(o[0], major) + hop_minor * hops(o[1], minor), o))


def turned(me, count, minor):
    major = count // minor
    high, low = lax.div(me, minor), lax.rem(me, minor)
    highs = [lax.rem(high + step, major) * minor for step in range(major)]
    lows = [lax.rem(low + step, minor) for step in range(minor)]
    return highs, lows


def kernel(
    rows, cols, piece, side,
    positions_hbm, types_hbm, alphas_hbm, omegas_hbm, radii_hbm, frequencies_hbm, field_hbm, start_hbm,
    out_ref,
    positions, types, alphas, omegas, radii, frequencies, field, start,
    gathered, partial, landed, sites, mates, own_sites, columns, coupling, col_sums, row_sums,
    load_sem, gather_send, gather_recv, sites_send, sites_recv, fold_send, fold_recv,
    mates_send, mates_recv, sum_send, sum_recv,
):
    nfreq, ntypes = frequencies.shape[0], alphas.shape[0]
    row, col = lax.axis_index("row"), lax.axis_index("col")
    tiles = rows // TILE
    group = LANES // piece
    depth = TILE * piece

    loads = [
        pltpu.make_async_copy(source, target, load_sem.at[number])
        for number, (source, target) in enumerate((
            (positions_hbm, positions), (types_hbm, types), (alphas_hbm, alphas), (omegas_hbm, omegas),
            (radii_hbm, radii), (frequencies_hbm, frequencies), (field_hbm, field), (start_hbm, start),
        ))
    ]
    barrier = pltpu.get_barrier_semaphore()

    row_offsets = nearest_first(rows, ROW_MINOR, 1)
    col_offsets = nearest_first(cols, COL_MINOR, 0.5)
    row_high, row_low = turned(row, rows, ROW_MINOR)
    col_high, col_low = turned(col, cols, COL_MINOR)

    def row_peer(slot, sign):
        far, near = row_offsets[slot]
        return (row_high[sign * far % len(row_high)] + row_low[sign * near % len(row_low)], col)

    def col_peer(slot, sign):
        far, near = col_offsets[slot]
        return (row, col_high[sign * far % len(col_high)] + col_low[sign * near % len(col_low)])

    row_order = range(rows - 1, 0, -1)
    col_order = range(cols - 1, 0, -1)

    reach_row = [hops(far, len(row_high)) + hops(near, len(row_low)) for far, near in row_offsets]
    reach_col = [hops(far, len(col_high)) for far, _ in col_offsets]
    everyone = sorted(
        [(-reach_row[slot], False, -slot) for slot in row_order]
        + [(-reach_col[slot] - COL_FIRST, True, -slot) for slot in col_order]
    )

    with jax.named_scope("greet"):
        for _, along_col, slot in everyone:
            peer = col_peer(-slot, 1) if along_col else row_peer(-slot, 1)
            pl.semaphore_signal(barrier, inc=1, device_id=peer, device_id_type=MESH)

    for load in loads:
        load.start()

    def send_row(source_of, target, send_sem, recv_sem, sign, slots=row_order, height=None):
        for slot in slots:
            pltpu.make_async_remote_copy(
                src_ref=source_of(slot), dst_ref=target.at[slot] if height is None else target.at[slot, pl.ds(0, height)],
                send_sem=send_sem, recv_sem=recv_sem,
                device_id=row_peer(slot, sign), device_id_type=MESH,
            ).start()

    def send_col(source, target, send_sem, recv_sem, slots=col_order):
        for slot in slots:
            pltpu.make_async_remote_copy(
                src_ref=source, dst_ref=target.at[slot], send_sem=send_sem, recv_sem=recv_sem,
                device_id=col_peer(slot, -1), device_id_type=MESH,
            ).start()

    def wait_for(buffer, count, sem, height=None):
        view = buffer.at[pl.ds(0, count)] if height is None else buffer.at[pl.ds(0, count), pl.ds(0, height)]
        pltpu.make_async_copy(view, view, sem).wait()

    def packed(ref):
        return jnp.concatenate([ref[0], ref[1], ref[2]], axis=1)

    with jax.named_scope("load"):
        for load in loads:
            load.wait()
    lane = lax.broadcasted_iota(jnp.int32, (nfreq, LANES), 1)
    level = lax.broadcasted_iota(jnp.int32, (nfreq, LANES), 0)
    kinds = types[...]
    radius = pick(kinds, radii, ntypes)
    place = positions[...] * side
    pad = jnp.zeros((nfreq - 4, piece), F32)
    site = jnp.concatenate([place, radius, pad], axis=0)
    start_packed = packed(start)
    message = jnp.concatenate([start_packed, site], axis=1)
    gathered[0, 0] = message
    sites[0] = message
    with jax.named_scope("barrier"):
        pl.semaphore_wait(barrier, rows + cols - 2)
    with jax.named_scope("first send"):
        for _, along_col, slot in everyone:
            if along_col:
                send_col(gathered.at[0, 0], gathered.at[0], gather_send.at[0], gather_recv.at[0], (-slot,))
            else:
                send_row(lambda _: sites.at[0, pl.ds(0, 4)], sites, sites_send, sites_recv, -1, (-slot,), 4)

    kinds_packed = jnp.broadcast_to(jnp.concatenate([kinds] * group, axis=1), (nfreq, LANES))
    omega = pick(kinds_packed, omegas, ntypes)
    alpha = pick(kinds_packed, alphas, ntypes)
    ratio = pick(level, frequencies, nfreq) / omega
    diagonal = (1.0 + ratio * ratio) / alpha
    inverse_diagonal = alpha / (1.0 + ratio * ratio)
    zeros_tail = jnp.zeros((nfreq, LANES - 3 * piece), F32)
    start_full = jnp.concatenate([start_packed, zeros_tail], axis=1)
    field_full = jnp.concatenate([packed(field), zeros_tail], axis=1)
    source_full = field_full - diagonal * start_full

    def total_of(values):
        while len(values) > 1:
            values = [sum(values[k:k + 2]) for k in range(0, len(values), 2)]
        return values[0]

    def unpack(block_of, count):
        blocks = [block_of(s) for s in range(count)]
        return [
            jnp.concatenate(
                [
                    jnp.concatenate([blocks[t + q][:, a * piece:(a + 1) * piece] for q in range(group)], axis=1)
                    for t in range(0, count, group)
                ],
                axis=1,
            )
            for a in range(3)
        ]

    def prepare():
        for c in range(cols):
            across = gathered[0, c].T[3 * piece:, :]
            for q in range(4):
                columns[q, c * piece:(c + 1) * piece, :] = jnp.broadcast_to(across[:, q:q + 1], (piece, LANES))

    def place_sites():
        for r in range(rows):
            own_sites[:, r * piece:(r + 1) * piece] = sites[r, :4, 3 * piece:]

    apart = (
        lax.broadcasted_iota(jnp.int32, (piece, LANES), 0) != lax.broadcasted_iota(jnp.int32, (piece, LANES), 1)
    )

    def build(chunk):
        for c in range(cols):
            base = slice(c * piece, (c + 1) * piece)
            column = [columns[q, base, :] for q in range(4)]
            for n in range(depth // LANES):
                span = slice(n * LANES, (n + 1) * LANES)
                place = slice(chunk * depth + n * LANES, chunk * depth + (n + 1) * LANES)
                offset = [column[q] - own_sites[q:q + 1, place] for q in range(3)]
                reach = column[3] + own_sites[3:4, place]
                square = offset[0] * offset[0] + offset[1] * offset[1] + offset[2] * offset[2] + reach * reach
                inverse = lax.rsqrt(square)
                second = inverse * inverse
                cube = second * inverse
                fifth = -3.0 * (cube * second)
                weighted = [offset[q] * fifth for q in range(3)]
                for number, (a, b) in enumerate(PAIRS):
                    value = weighted[a] * offset[b]
                    if a == b:
                        value = value + cube
                    if chunk == 0 and c == 0 and n == 0:
                        value = jnp.where(apart, value, 0.0)
                    high = value.astype(BF16)
                    coupling[chunk, number, 0, base, span] = high
                    coupling[chunk, number, 1, base, span] = (value - high.astype(F32)).astype(BF16)

    def contract(chunk, lefts):
        out = [None] * 3

        def add(a, value):
            out[a] = value if out[a] is None else out[a] + value

        def dot(left, number, part):
            return jnp.dot(left, coupling[chunk, number, part], preferred_element_type=F32)

        for number, (a, b) in enumerate(PAIRS):
            first, second = lefts[number]
            main, rest = dot(first, number, 0), dot(second, number, 1)
            add(a, main[:nfreq] + (main[nfreq:2 * nfreq] + rest[:nfreq]))
            if a != b:
                add(b, main[2 * nfreq:3 * nfreq] + (main[3 * nfreq:] + rest[nfreq:]))
        return out

    def apply(turn):
        with jax.named_scope("gather wait"):
            wait_for(gathered.at[turn], cols - 1, gather_recv.at[turn])
        if turn == 0:
            prepare()
            with jax.named_scope("sites wait"):
                wait_for(sites, rows - 1, sites_recv, 4)
            place_sites()
        outs = [None] * tiles
        with jax.named_scope("contract"):
            values = unpack(lambda s: gathered[turn, s], cols)
            highs = [value.astype(BF16).astype(F32) for value in values]
            lows = [value - high for value, high in zip(values, highs)]
            lefts = []
            for a, b in PAIRS:
                if a == b:
                    main, rest = [highs[a], lows[a]], [highs[a], lows[a]]
                else:
                    main, rest = [highs[b], lows[b], highs[a], lows[a]], [highs[b], highs[a]]
                lefts.append(tuple(jnp.concatenate(part, axis=0).astype(BF16) for part in (main, rest)))
            for chunk in range(tiles - 1, -1, -1):
                if turn == 0:
                    build(chunk)
                out = contract(chunk, lefts)
                outs[chunk] = out
                first = chunk * TILE
                low = jnp.concatenate([out[a][SHORT:] for a in range(3)] + [out[0][SHORT:]], axis=0)
                for s in range(TILE):
                    cut = slice(s * piece, (s + 1) * piece)
                    block = jnp.concatenate([out[0][:, cut], out[1][:, cut], out[2][:, cut], low[:, cut]], axis=1)
                    if first + s == 0:
                        landed[turn, 0] = block
                    else:
                        partial[turn, first + s] = block
                send_row(
                    lambda slot: partial.at[turn, slot, pl.ds(0, SHORT)], landed.at[turn], fold_send.at[turn],
                    fold_recv.at[turn], 1, range(first + TILE - 1, max(first - 1, 0), -1), SHORT,
                )
        return outs

    def folded(turn):
        with jax.named_scope("fold wait"):
            wait_for(landed.at[turn], rows - 1, fold_recv.at[turn], SHORT)
        total = total_of([landed[turn, r, :SHORT] for r in range(rows)])
        parts = [
            jnp.concatenate(
                [total[:, a * piece:(a + 1) * piece], total[a * (nfreq - SHORT):(a + 1) * (nfreq - SHORT), 3 * piece:]], axis=0
            )
            for a in range(3)
        ]
        return jnp.concatenate(parts + [zeros_tail], axis=1)

    def spread(turn, value):
        gathered[turn, 0] = value
        with jax.named_scope("gather send"):
            send_col(gathered.at[turn, 0], gathered.at[turn], gather_send.at[turn], gather_recv.at[turn])

    apply(0)
    powers = [source_full - folded(0)]
    scaled = []
    for turn in range(1, APPLICATIONS - 1):
        scaled.append(powers[-1] * inverse_diagonal)
        spread(turn, scaled[-1])
        apply(turn)
        powers.append(folded(turn))

    last = APPLICATIONS - 1
    scaled.append(powers[-1] * inverse_diagonal)
    spread(last, scaled[-1])
    mates[0] = scaled[-1]
    send_row(lambda slot: mates.at[0], mates, mates_send, mates_recv, -1)
    moments = jnp.zeros((nfreq, LANES), F32)
    for k, (i, j) in enumerate(MOMENTS):
        local = jnp.sum(scaled[i] * powers[j], axis=1, keepdims=True)
        moments = jnp.where(lane == k, local, moments)
    outs = apply(last)
    with jax.named_scope("mates wait"):
        wait_for(mates, rows - 1, mates_recv)
    terms = []
    for chunk in range(tiles):
        own = unpack(lambda s: mates[chunk * TILE + s], TILE)
        terms += [own[a] * outs[chunk][a] for a in range(3)]
    local = jnp.sum(total_of(terms), axis=1, keepdims=True)
    moments = jnp.where(lane == len(MOMENTS), local, moments)
    with jax.named_scope("sum"):
        spaced = pltpu.roll(moments, 0, 1, stride=LANES // nfreq, stride_axis=0)
        col_sums[0] = jnp.sum(spaced, axis=0, keepdims=True)
        send_col(col_sums.at[0], col_sums, sum_send.at[0], sum_recv.at[0])
        wait_for(col_sums, cols - 1, sum_recv.at[0])
        row_sums[0] = total_of([col_sums[c] for c in range(cols)])
        send_row(lambda slot: row_sums.at[0], row_sums, sum_send.at[1], sum_recv.at[1], -1)
        powers.append(folded(last))
        wait_for(row_sums, rows - 1, sum_recv.at[1])
    total = jnp.broadcast_to(total_of([row_sums[r] for r in range(rows)]), (nfreq, LANES))
    column_of = lane - level * (LANES // nfreq)

    m = [jnp.sum(jnp.where(column_of == k, total, 0.0), axis=1, keepdims=True) for k in range(len(MOMENTS) + 1)]
    a0 = m[1] / m[0]
    h0 = m[0]
    h1 = m[2] - a0 * m[1]
    a1 = (m[3] - 2.0 * a0 * m[2] + a0 * a0 * m[1]) / h1
    b1 = h1 / h0
    c1 = -(a0 + a1)
    c0 = a0 * a1 - b1
    h2 = m[4] + c1 * m[3] + c0 * m[2]
    a2 = (m[5] + c1 * m[4] + c0 * m[3]) / h2 + c1
    b2 = h2 / h1
    e2 = c1 - a2
    e1 = c0 - a2 * c1 - b2
    e0 = b2 * a0 - a2 * c0
    top = 1.0 / (e2 - 1.0 - e1 + e0)
    p3, p2, p1, p0 = top, e2 * top, e1 * top, e0 * top
    s2 = -p3
    s1 = -p2 - s2
    s0 = -p1 - s1
    residual = p0 * powers[0] + p1 * powers[1] + p2 * powers[2] + p3 * powers[3]
    dipoles = start_full + (s0 * scaled[0] + s1 * scaled[1] + s2 * scaled[2])
    for a in range(3):
        out_ref[0, a] = dipoles[:, a * piece:(a + 1) * piece]
        out_ref[1, a] = residual[:, a * piece:(a + 1) * piece]

    for turn in range(APPLICATIONS):
        wait_for(gathered.at[turn], cols - 1, gather_send.at[turn])
        wait_for(landed.at[turn], rows - 1, fold_send.at[turn], SHORT)
    wait_for(sites, rows - 1, sites_send, 4)
    wait_for(mates, rows - 1, mates_send)
    wait_for(col_sums, cols - 1, sum_send.at[0])
    wait_for(row_sums, rows - 1, sum_send.at[1])


def solution(mesh):
    rows, cols = mesh.shape["row"], mesh.shape["col"]

    def shards(positions, atom_types, alpha_table, omega_table, radius_table, frequencies, field, start_dipoles):
        piece, nfreq = positions.shape[1], frequencies.shape[0]
        side = (10.0 * piece * rows * cols) ** (1.0 / 3.0)
        operands = (
            positions, atom_types.reshape(1, piece), alpha_table, omega_table, radius_table, frequencies,
            field, start_dipoles,
        )
        vmem = pl.BlockSpec(memory_space=pltpu.VMEM)
        tile = (nfreq, LANES)
        dma = pltpu.SemaphoreType.DMA
        places = [pltpu.VMEM] * 2 + [pltpu.SMEM] * 4 + [pltpu.VMEM] * 2
        both = pl.pallas_call(
            functools.partial(kernel, rows, cols, piece, side),
            out_shape=pltpu.VMEM((2,) + field.shape, F32),
            in_specs=[pl.BlockSpec(memory_space=pltpu.HBM)] * len(operands),
            out_specs=vmem,
            scratch_shapes=[space(array.shape, array.dtype) for space, array in zip(places, operands)] + [
                pltpu.VMEM((APPLICATIONS, cols) + tile, F32),
                pltpu.VMEM((APPLICATIONS, rows) + tile, F32),
                pltpu.VMEM((APPLICATIONS, rows) + tile, F32),
                pltpu.VMEM((rows,) + tile, F32),
                pltpu.VMEM((rows,) + tile, F32),
                pltpu.VMEM((4, rows * piece), F32),
                pltpu.VMEM((4, cols * piece, LANES), F32),
                pltpu.VMEM((rows // TILE, len(PAIRS), 2, cols * piece, TILE * piece), BF16),
                pltpu.VMEM((cols, 1, LANES), F32),
                pltpu.VMEM((rows, 1, LANES), F32),
                dma((len(operands),)),
                dma((APPLICATIONS,)), dma((APPLICATIONS,)),
                dma, dma,
                dma((APPLICATIONS,)), dma((APPLICATIONS,)),
                dma, dma,
                dma((2,)), dma((2,)),
            ],
            compiler_params=pltpu.CompilerParams(
                collective_id=0, has_side_effects=True, vmem_limit_bytes=60 * 1024 * 1024
            ),
        )(*operands)
        return both[0], both[1]

    placed = (
        P(None, ("row", "col")),
        P(("row", "col")),
        P(),
        P(),
        P(),
        P(),
        P(None, None, ("row", "col")),
        P(None, None, ("row", "col")),
    )
    return jax.shard_map(
        shards,
        mesh=mesh,
        in_specs=placed,
        out_specs=(P(None, None, ("row", "col")), P(None, None, ("row", "col"))),
        check_vma=False,
    )
```

```python
import functools

import jax
import jax.numpy as jnp
from jax import lax
from jax.experimental import pallas as pl
from jax.experimental.pallas import tpu as pltpu
from jax.sharding import PartitionSpec as P

MESH = pl.DeviceIdType.MESH
F32, BF16 = jnp.float32, jnp.bfloat16
APPLICATIONS = 4
PAIRS = ((0, 0), (1, 1), (2, 2), (0, 1), (0, 2), (1, 2))
LANES = 128
TILE = 8
SHORT = 6
ROW_MINOR = 4
COL_MINOR = 2
COL_FIRST = 1
MOMENTS = ((0, 0), (0, 1), (1, 1), (1, 2), (2, 2))


def pick(indices, table, count):
    value = jnp.full(indices.shape, table[0], F32)
    for number in range(1, count):
        value = jnp.where(indices == number, table[number], value)
    return value


def hops(step, length):
    return min(step, length - step)


def nearest_first(count, minor, hop_minor):
    major = count // minor
    offsets = [(far, near) for far in range(major) for near in range(minor)]
    return sorted(offsets, key=lambda o: (hops(o[0], major) + hop_minor * hops(o[1], minor), o))


def turned(me, count, minor):
    major = count // minor
    high, low = lax.div(me, minor), lax.rem(me, minor)
    highs = [lax.rem(high + step, major) * minor for step in range(major)]
    lows = [lax.rem(low + step, minor) for step in range(minor)]
    return highs, lows


def kernel(
    rows, cols, piece, side,
    positions_hbm, types_hbm, alphas_hbm, omegas_hbm, radii_hbm, frequencies_hbm, field_hbm, start_hbm,
    out_ref,
    positions, types, alphas, omegas, radii, frequencies, field, start,
    gathered, partial, landed, sites, mates, own_sites, columns, coupling, col_sums, row_sums,
    load_sem, gather_send, gather_recv, sites_send, sites_recv, fold_send, fold_recv,
    mates_send, mates_recv, sum_send, sum_recv,
):
    nfreq, ntypes = frequencies.shape[0], alphas.shape[0]
    row, col = lax.axis_index("row"), lax.axis_index("col")
    tiles = rows // TILE
    group = LANES // piece
    depth = TILE * piece

    loads = [
        pltpu.make_async_copy(source, target, load_sem.at[number])
        for number, (source, target) in enumerate((
            (positions_hbm, positions), (types_hbm, types), (alphas_hbm, alphas), (omegas_hbm, omegas),
            (radii_hbm, radii), (frequencies_hbm, frequencies), (field_hbm, field), (start_hbm, start),
        ))
    ]
    barrier = pltpu.get_barrier_semaphore()

    row_offsets = nearest_first(rows, ROW_MINOR, 1)
    col_offsets = nearest_first(cols, COL_MINOR, 0.5)
    row_high, row_low = turned(row, rows, ROW_MINOR)
    col_high, col_low = turned(col, cols, COL_MINOR)

    def row_peer(slot, sign):
        far, near = row_offsets[slot]
        return (row_high[sign * far % len(row_high)] + row_low[sign * near % len(row_low)], col)

    def col_peer(slot, sign):
        far, near = col_offsets[slot]
        return (row, col_high[sign * far % len(col_high)] + col_low[sign * near % len(col_low)])

    row_order = range(rows - 1, 0, -1)
    col_order = range(cols - 1, 0, -1)

    reach_row = [hops(far, len(row_high)) + hops(near, len(row_low)) for far, near in row_offsets]
    reach_col = [hops(far, len(col_high)) for far, _ in col_offsets]
    everyone = sorted(
        [(-reach_row[slot], False, -slot) for slot in row_order]
        + [(-reach_col[slot] - COL_FIRST, True, -slot) for slot in col_order]
    )

    with jax.named_scope("greet"):
        for _, along_col, slot in everyone:
            peer = col_peer(-slot, 1) if along_col else row_peer(-slot, 1)
            pl.semaphore_signal(barrier, inc=1, device_id=peer, device_id_type=MESH)

    for load in loads:
        load.start()

    def send_row(source_of, target, send_sem, recv_sem, sign, slots=row_order, height=None):
        for slot in slots:
            pltpu.make_async_remote_copy(
                src_ref=source_of(slot), dst_ref=target.at[slot] if height is None else target.at[slot, pl.ds(0, height)],
                send_sem=send_sem, recv_sem=recv_sem,
                device_id=row_peer(slot, sign), device_id_type=MESH,
            ).start()

    def send_col(source, target, send_sem, recv_sem, slots=col_order):
        for slot in slots:
            pltpu.make_async_remote_copy(
                src_ref=source, dst_ref=target.at[slot], send_sem=send_sem, recv_sem=recv_sem,
                device_id=col_peer(slot, -1), device_id_type=MESH,
            ).start()

    def wait_for(buffer, count, sem, height=None):
        view = buffer.at[pl.ds(0, count)] if height is None else buffer.at[pl.ds(0, count), pl.ds(0, height)]
        pltpu.make_async_copy(view, view, sem).wait()

    def packed(ref):
        return jnp.concatenate([ref[0], ref[1], ref[2]], axis=1)

    with jax.named_scope("load"):
        for load in loads:
            load.wait()
    lane = lax.broadcasted_iota(jnp.int32, (nfreq, LANES), 1)
    level = lax.broadcasted_iota(jnp.int32, (nfreq, LANES), 0)
    kinds = types[...]
    radius = pick(kinds, radii, ntypes)
    place = positions[...] * side
    pad = jnp.zeros((nfreq - 4, piece), F32)
    site = jnp.concatenate([place, radius, pad], axis=0)
    start_packed = packed(start)
    message = jnp.concatenate([start_packed, site], axis=1)
    gathered[0, 0] = message
    sites[0] = message
    with jax.named_scope("barrier"):
        pl.semaphore_wait(barrier, rows + cols - 2)
    with jax.named_scope("first send"):
        for _, along_col, slot in everyone:
            if along_col:
                send_col(gathered.at[0, 0], gathered.at[0], gather_send.at[0], gather_recv.at[0], (-slot,))
            else:
                send_row(lambda _: sites.at[0, pl.ds(0, 4)], sites, sites_send, sites_recv, -1, (-slot,), 4)

    kinds_packed = jnp.broadcast_to(jnp.concatenate([kinds] * group, axis=1), (nfreq, LANES))
    omega = pick(kinds_packed, omegas, ntypes)
    alpha = pick(kinds_packed, alphas, ntypes)
    ratio = pick(level, frequencies, nfreq) / omega
    diagonal = (1.0 + ratio * ratio) / alpha
    inverse_diagonal = alpha / (1.0 + ratio * ratio)
    zeros_tail = jnp.zeros((nfreq, LANES - 3 * piece), F32)
    start_full = jnp.concatenate([start_packed, zeros_tail], axis=1)
    field_full = jnp.concatenate([packed(field), zeros_tail], axis=1)
    source_full = field_full - diagonal * start_full

    def total_of(values):
        while len(values) > 1:
            values = [sum(values[k:k + 2]) for k in range(0, len(values), 2)]
        return values[0]

    def unpack(block_of, count):
        blocks = [block_of(s) for s in range(count)]
        return [
            jnp.concatenate(
                [
                    jnp.concatenate([blocks[t + q][:, a * piece:(a + 1) * piece] for q in range(group)], axis=1)
                    for t in range(0, count, group)
                ],
                axis=1,
            )
            for a in range(3)
        ]

    def prepare():
        for c in range(cols):
            across = gathered[0, c].T[3 * piece:, :]
            for q in range(4):
                columns[q, c * piece:(c + 1) * piece, :] = jnp.broadcast_to(across[:, q:q + 1], (piece, LANES))

    def place_sites():
        for r in range(rows):
            own_sites[:, r * piece:(r + 1) * piece] = sites[r, :4, 3 * piece:]

    apart = (
        lax.broadcasted_iota(jnp.int32, (piece, LANES), 0) != lax.broadcasted_iota(jnp.int32, (piece, LANES), 1)
    )

    def build(chunk):
        for c in range(cols):
            base = slice(c * piece, (c + 1) * piece)
            column = [columns[q, base, :] for q in range(4)]
            for n in range(depth // LANES):
                span = slice(n * LANES, (n + 1) * LANES)
                place = slice(chunk * depth + n * LANES, chunk * depth + (n + 1) * LANES)
                offset = [column[q] - own_sites[q:q + 1, place] for q in range(3)]
                reach = column[3] + own_sites[3:4, place]
                square = offset[0] * offset[0] + offset[1] * offset[1] + offset[2] * offset[2] + reach * reach
                inverse = lax.rsqrt(square)
                second = inverse * inverse
                cube = second * inverse
                fifth = -3.0 * (cube * second)
                weighted = [offset[q] * fifth for q in range(3)]
                for number, (a, b) in enumerate(PAIRS):
                    value = weighted[a] * offset[b]
                    if a == b:
                        value = value + cube
                    if chunk == 0 and c == 0 and n == 0:
                        value = jnp.where(apart, value, 0.0)
                    high = value.astype(BF16)
                    coupling[chunk, number, 0, base, span] = high
                    coupling[chunk, number, 1, base, span] = (value - high.astype(F32)).astype(BF16)

    def contract(chunk, lefts):
        out = [None] * 3

        def add(a, value):
            out[a] = value if out[a] is None else out[a] + value

        def dot(left, number, part):
            return jnp.dot(left, coupling[chunk, number, part], preferred_element_type=F32)

        for number, (a, b) in enumerate(PAIRS):
            first, second = lefts[number]
            main, rest = dot(first, number, 0), dot(second, number, 1)
            add(a, main[:nfreq] + (main[nfreq:2 * nfreq] + rest[:nfreq]))
            if a != b:
                add(b, main[2 * nfreq:3 * nfreq] + (main[3 * nfreq:] + rest[nfreq:]))
        return out

    def send_chunk(turn, chunk, out):
        first = chunk * TILE
        low = jnp.concatenate([out[a][SHORT:] for a in range(3)] + [out[0][SHORT:]], axis=0)
        for s in range(TILE):
            cut = slice(s * piece, (s + 1) * piece)
            block = jnp.concatenate([out[0][:, cut], out[1][:, cut], out[2][:, cut], low[:, cut]], axis=1)
            if first + s == 0:
                landed[turn, 0] = block
            else:
                partial[turn, first + s] = block
        send_row(
            lambda slot: partial.at[turn, slot, pl.ds(0, SHORT)], landed.at[turn], fold_send.at[turn],
            fold_recv.at[turn], 1, range(first + TILE - 1, max(first - 1, 0), -1), SHORT,
        )

    def apply(turn):
        with jax.named_scope("gather wait"):
            wait_for(gathered.at[turn], cols - 1, gather_recv.at[turn])
        if turn == 0:
            prepare()
            with jax.named_scope("sites wait"):
                wait_for(sites, rows - 1, sites_recv, 4)
            place_sites()
        outs = [None] * tiles
        with jax.named_scope("contract"):
            values = unpack(lambda s: gathered[turn, s], cols)
            highs = [value.astype(BF16).astype(F32) for value in values]
            lows = [value - high for value, high in zip(values, highs)]
            lefts = []
            for a, b in PAIRS:
                if a == b:
                    main, rest = [highs[a], lows[a]], [highs[a], lows[a]]
                else:
                    main, rest = [highs[b], lows[b], highs[a], lows[a]], [highs[b], highs[a]]
                lefts.append(tuple(jnp.concatenate(part, axis=0).astype(BF16) for part in (main, rest)))
            for chunk in range(tiles - 1, -1, -1):
                if turn == 0:
                    build(chunk)
                if 0 < turn < APPLICATIONS - 1 and chunk >= tiles - 1:
                    @pl.when(row >= 0)
                    def _():
                        send_chunk(turn, chunk, contract(chunk, lefts))
                else:
                    outs[chunk] = contract(chunk, lefts)
                    send_chunk(turn, chunk, outs[chunk])
        return outs

    def folded(turn):
        with jax.named_scope("fold wait"):
            wait_for(landed.at[turn], rows - 1, fold_recv.at[turn], SHORT)
        total = total_of([landed[turn, r, :SHORT] for r in range(rows)])
        parts = [
            jnp.concatenate(
                [total[:, a * piece:(a + 1) * piece], total[a * (nfreq - SHORT):(a + 1) * (nfreq - SHORT), 3 * piece:]], axis=0
            )
            for a in range(3)
        ]
        return jnp.concatenate(parts + [zeros_tail], axis=1)

    def spread(turn, value):
        gathered[turn, 0] = value
        with jax.named_scope("gather send"):
            send_col(gathered.at[turn, 0], gathered.at[turn], gather_send.at[turn], gather_recv.at[turn])

    apply(0)
    powers = [source_full - folded(0)]
    scaled = []
    for turn in range(1, APPLICATIONS - 1):
        scaled.append(powers[-1] * inverse_diagonal)
        spread(turn, scaled[-1])
        apply(turn)
        powers.append(folded(turn))

    last = APPLICATIONS - 1
    scaled.append(powers[-1] * inverse_diagonal)
    spread(last, scaled[-1])
    mates[0] = scaled[-1]
    send_row(lambda slot: mates.at[0], mates, mates_send, mates_recv, -1)
    moments = jnp.zeros((nfreq, LANES), F32)
    for k, (i, j) in enumerate(MOMENTS):
        local = jnp.sum(scaled[i] * powers[j], axis=1, keepdims=True)
        moments = jnp.where(lane == k, local, moments)
    outs = apply(last)
    with jax.named_scope("mates wait"):
        wait_for(mates, rows - 1, mates_recv)
    terms = []
    for chunk in range(tiles):
        own = unpack(lambda s: mates[chunk * TILE + s], TILE)
        terms += [own[a] * outs[chunk][a] for a in range(3)]
    local = jnp.sum(total_of(terms), axis=1, keepdims=True)
    moments = jnp.where(lane == len(MOMENTS), local, moments)
    with jax.named_scope("sum"):
        spaced = pltpu.roll(moments, 0, 1, stride=LANES // nfreq, stride_axis=0)
        col_sums[0] = jnp.sum(spaced, axis=0, keepdims=True)
        send_col(col_sums.at[0], col_sums, sum_send.at[0], sum_recv.at[0])
        wait_for(col_sums, cols - 1, sum_recv.at[0])
        row_sums[0] = total_of([col_sums[c] for c in range(cols)])
        send_row(lambda slot: row_sums.at[0], row_sums, sum_send.at[1], sum_recv.at[1], -1)
        powers.append(folded(last))
        wait_for(row_sums, rows - 1, sum_recv.at[1])
    total = jnp.broadcast_to(total_of([row_sums[r] for r in range(rows)]), (nfreq, LANES))
    column_of = lane - level * (LANES // nfreq)

    m = [jnp.sum(jnp.where(column_of == k, total, 0.0), axis=1, keepdims=True) for k in range(len(MOMENTS) + 1)]
    a0 = m[1] / m[0]
    h0 = m[0]
    h1 = m[2] - a0 * m[1]
    a1 = (m[3] - 2.0 * a0 * m[2] + a0 * a0 * m[1]) / h1
    b1 = h1 / h0
    c1 = -(a0 + a1)
    c0 = a0 * a1 - b1
    h2 = m[4] + c1 * m[3] + c0 * m[2]
    a2 = (m[5] + c1 * m[4] + c0 * m[3]) / h2 + c1
    b2 = h2 / h1
    e2 = c1 - a2
    e1 = c0 - a2 * c1 - b2
    e0 = b2 * a0 - a2 * c0
    top = 1.0 / (e2 - 1.0 - e1 + e0)
    p3, p2, p1, p0 = top, e2 * top, e1 * top, e0 * top
    s2 = -p3
    s1 = -p2 - s2
    s0 = -p1 - s1
    residual = p0 * powers[0] + p1 * powers[1] + p2 * powers[2] + p3 * powers[3]
    dipoles = start_full + (s0 * scaled[0] + s1 * scaled[1] + s2 * scaled[2])
    for a in range(3):
        out_ref[0, a] = dipoles[:, a * piece:(a + 1) * piece]
        out_ref[1, a] = residual[:, a * piece:(a + 1) * piece]

    for turn in range(APPLICATIONS):
        wait_for(gathered.at[turn], cols - 1, gather_send.at[turn])
        wait_for(landed.at[turn], rows - 1, fold_send.at[turn], SHORT)
    wait_for(sites, rows - 1, sites_send, 4)
    wait_for(mates, rows - 1, mates_send)
    wait_for(col_sums, cols - 1, sum_send.at[0])
    wait_for(row_sums, rows - 1, sum_send.at[1])


def solution(mesh):
    rows, cols = mesh.shape["row"], mesh.shape["col"]

    def shards(positions, atom_types, alpha_table, omega_table, radius_table, frequencies, field, start_dipoles):
        piece, nfreq = positions.shape[1], frequencies.shape[0]
        side = (10.0 * piece * rows * cols) ** (1.0 / 3.0)
        operands = (
            positions, atom_types.reshape(1, piece), alpha_table, omega_table, radius_table, frequencies,
            field, start_dipoles,
        )
        vmem = pl.BlockSpec(memory_space=pltpu.VMEM)
        tile = (nfreq, LANES)
        dma = pltpu.SemaphoreType.DMA
        places = [pltpu.VMEM] * 2 + [pltpu.SMEM] * 4 + [pltpu.VMEM] * 2
        both = pl.pallas_call(
            functools.partial(kernel, rows, cols, piece, side),
            out_shape=pltpu.VMEM((2,) + field.shape, F32),
            in_specs=[pl.BlockSpec(memory_space=pltpu.HBM)] * len(operands),
            out_specs=vmem,
            scratch_shapes=[space(array.shape, array.dtype) for space, array in zip(places, operands)] + [
                pltpu.VMEM((APPLICATIONS, cols) + tile, F32),
                pltpu.VMEM((APPLICATIONS, rows) + tile, F32),
                pltpu.VMEM((APPLICATIONS, rows) + tile, F32),
                pltpu.VMEM((rows,) + tile, F32),
                pltpu.VMEM((rows,) + tile, F32),
                pltpu.VMEM((4, rows * piece), F32),
                pltpu.VMEM((4, cols * piece, LANES), F32),
                pltpu.VMEM((rows // TILE, len(PAIRS), 2, cols * piece, TILE * piece), BF16),
                pltpu.VMEM((cols, 1, LANES), F32),
                pltpu.VMEM((rows, 1, LANES), F32),
                dma((len(operands),)),
                dma((APPLICATIONS,)), dma((APPLICATIONS,)),
                dma, dma,
                dma((APPLICATIONS,)), dma((APPLICATIONS,)),
                dma, dma,
                dma((2,)), dma((2,)),
            ],
            compiler_params=pltpu.CompilerParams(
                collective_id=0, has_side_effects=True, vmem_limit_bytes=60 * 1024 * 1024
            ),
        )(*operands)
        return both[0], both[1]

    placed = (
        P(None, ("row", "col")),
        P(("row", "col")),
        P(),
        P(),
        P(),
        P(),
        P(None, None, ("row", "col")),
        P(None, None, ("row", "col")),
    )
    return jax.shard_map(
        shards,
        mesh=mesh,
        in_specs=placed,
        out_specs=(P(None, None, ("row", "col")), P(None, None, ("row", "col"))),
        check_vma=False,
    )
```
